256 devices in a mesh: ta: 32 (over z, y_hi, core), gx: 8 (over y_lo, x).
Axes of the slice: x: 4, y: 4 (y_hi: 2, y_lo: 2; y = y_hi * 2 + y_lo), z: 8, core: 2. Of those that a mesh axis runs over, the one named last changes fastest.
Arguments:
- link_angles: float32 [4, 64, 32, 256], P(None, 'ta', 'gx'), may hold values from -3.140625 to 3.140625
- cotangent: float32 [4, 64, 32, 256], P(None, 'ta', 'gx'), may hold values from -14 to 14
- square_weight: float32 [3, 6], replicated, may hold values from 0.3 to 1.5
- oblong_weight: float32 [3, 12], replicated, may hold values from -0.5 to 0.5
Outputs:
- link_cotangent: float32 [4, 64, 32, 256], P(None, 'ta', 'gx')
- square_gradient: float32 [3, 6], replicated
- oblong_gradient: float32 [3, 12], replicated
The draws below stay inside these ranges and needn't reach their ends.
All inputs are finite; a program needn't handle non-finite values.
Results may differ from the reference program's by a relative error of at most 0.0003.
Values sent between devices are 32-bit elements; how exact they have to be, the bound alone decides.
No kernel may reach another device: no remote copies, remote signals or barrier semaphores. Data moves between devices by JAX's collectives and lax.ppermute only.
A program may use at most 192 MiB of HBM per device.

```python
import math
import jax
import jax.numpy as jnp
from jax import lax

Y = 16
Z = 16
STEPS = 3
NT = 64
NX = 32
SITES = 524288


def draw_cotangent(key, part):
    key = jax.random.fold_in(key, 11)
    shape = (4, NT, NX, Y * Z)
    ramp = 1.0 + 2.0 * jnp.arange(NT, dtype=jnp.float32)[None, :, None, None] / max(NT - 1, 1)
    base = jnp.clip(jax.random.normal(key, shape, jnp.float32), -4.0, 4.0)
    return (base * ramp).astype(jnp.float32)


def setup_inputs(seed: int = 0) -> dict:
    seeds = jax.random.split(jax.random.key(seed), 5)
    link_angles = jnp.clip(jax.random.uniform(seeds[0], (4, NT, NX, Y * Z), jnp.float32, -3.140625, 3.140625), -3.140625, 3.140625)
    cotangent = draw_cotangent(jax.random.fold_in(seeds[4], 71), 0)
    square_weight = jnp.clip(jnp.exp(jax.random.uniform(seeds[2], (STEPS, 6), jnp.float32, math.log(0.3), math.log(1.5))), 0.3, 1.5)
    oblong_weight = jnp.clip(jax.random.uniform(seeds[3], (STEPS, 12), jnp.float32, -0.5, 0.5), -0.5, 0.5)
    return {"link_angles": link_angles, "cotangent": cotangent, "square_weight": square_weight, "oblong_weight": oblong_weight}


flow_step = 0.05

def unit_vector(direction, length):
    return tuple((length * int(place == direction) for place in range(4)))

def add_vectors(first, second):
    return tuple((first[place] + second[place] for place in range(4)))

def square_loops():
    loops = []
    for first in range(4):
        for second in range(first + 1, 4):
            none = (0, 0, 0, 0)
            loops.append([(first, none, 1.0), (second, unit_vector(first, 1), 1.0), (first, unit_vector(second, 1), -1.0), (second, none, -1.0)])
    return loops

def oblong_loops():
    loops = []
    for first in range(4):
        for second in range(4):
            if second != first:
                none = (0, 0, 0, 0)
                loops.append([(first, none, 1.0), (first, unit_vector(first, 1), 1.0), (second, unit_vector(first, 2), 1.0), (first, add_vectors(unit_vector(first, 1), unit_vector(second, 1)), -1.0), (first, unit_vector(second, 1), -1.0), (second, none, -1.0)])
    return loops

def shifted(field, direction, amount):
    if amount == 0:
        return field
    if direction == 0:
        return jnp.roll(field, -amount, 0)
    if direction == 1:
        return jnp.roll(field, -amount, 1)
    if direction == 2:
        return jnp.roll(field, -amount * Z, 2)
    block = field.reshape(field.shape[0], field.shape[1], Y, Z)
    return jnp.roll(block, -amount, 3).reshape(field.shape)

def moved_by(field, offset, factor):
    for place in range(4):
        field = shifted(field, place, factor * offset[place])
    return field

def loop_angle(theta, loop):
    total = None
    for direction, offset, sign in loop:
        moved = moved_by(theta[direction], offset, 1)
        total = sign * moved if total is None else total + sign * moved
    return total

def drift(theta, square_row, oblong_row):
    pairs = [(square_row[index], loop) for index, loop in enumerate(square_loops())]
    pairs = pairs + [(oblong_row[index], loop) for index, loop in enumerate(oblong_loops())]
    parts = [jnp.zeros(theta.shape[1:], jnp.float32) for place in range(4)]
    for weight, loop in pairs:
        force = -weight * jnp.sin(loop_angle(theta, loop))
        for direction, offset, sign in loop:
            parts[direction] = parts[direction] + sign * moved_by(force, offset, -1)
    return jnp.stack(parts)

def one_step(state, rows):
    square_row, oblong_row = rows
    drift_zero = flow_step * drift(state, square_row, oblong_row)
    second = state + 0.25 * drift_zero
    drift_one = flow_step * drift(second, square_row, oblong_row)
    third = second + 8.0 / 9.0 * drift_one - 17.0 / 36.0 * drift_zero
    drift_two = flow_step * drift(third, square_row, oblong_row)
    return third + 0.75 * drift_two - 8.0 / 9.0 * drift_one + 17.0 / 36.0 * drift_zero

def flow(theta, square_weight, oblong_weight):
    stepper = jax.checkpoint(one_step)

    def advance(state, rows):
        return (stepper(state, rows), jnp.float32(0.0))
    final, unused = lax.scan(advance, theta, (square_weight, oblong_weight))
    return final

def reference(link_angles, cotangent, square_weight, oblong_weight):
    flowed, pullback = jax.vjp(flow, link_angles, square_weight, oblong_weight)
    link_cotangent, square_raw, oblong_raw = pullback(cotangent)
    scale = 1.0 / jnp.sqrt(jnp.float32(SITES))
    return (link_cotangent, square_raw * scale, oblong_raw * scale)
```

```python
import math

import jax
import jax.numpy as jnp
from jax import lax
from jax.experimental import pallas as pl
from jax.experimental.pallas import tpu as pltpu
from jax.sharding import PartitionSpec as P


Z = 16
STEPS = 3
STEP = 0.05
TURN = 2.0 * math.pi
PLANES = [(0, 1), (0, 2), (0, 3), (1, 2), (1, 3), (2, 3)]
BLOCK = 4
HALF = 128
F32 = jnp.float32

SIN = [6.283182621002197, -41.34142303466797, 81.59618377685547,
       -76.5801010131836, 41.20539093017578, -12.271258354187012]
COS = [1.0, -19.73920440673828, 64.93911743164062, -85.45016479492188,
       60.16783142089844, -25.968311309814453, 6.529608726501465]


def oblong_index(first, second):
    return first * 3 + second - int(second > first)


def home(tau, xi, core):
    return ((tau % 16) * 2 + core) * 8 + xi % 8


def place(tau, xi, core):
    p = (tau + 12) % 16
    z, y_hi = (p, 0) if p < 8 else (15 - p, 1)
    xi = xi % 8
    x, side = (xi, 0) if xi < 4 else (7 - xi, 1)
    y_lo = side if y_hi == 0 else 1 - side
    return (z * 4 + y_hi * 2 + core) * 8 + y_lo * 4 + x


EVERY = [(t, x, c) for t in range(16) for x in range(8) for c in range(2)]


def permute(array, source, start=place, end=place):
    pairs = [(start(*source(t, x, c)), end(t, x, c)) for t, x, c in EVERY]
    return lax.ppermute(array, ("ta", "gx"), pairs)


def swap_cores(array):
    return permute(array, lambda t, x, c: (t, x, 1 - c))


SOURCES = [((-1, 0), (1, 0)), ((0, -1), (0, 1)), ((-1, -1), (1, 1)), ((1, -1), (-1, 1))]


def exchange(block):
    parts = []
    for choices in SOURCES:
        def source(t, x, c, choices=choices):
            return (t + choices[c][0], x + choices[c][1], 1 - c)
        parts.append(permute(block, source))
    mine = jnp.concatenate(parts, 1)
    return mine, swap_cores(mine)


def lane(shape):
    return lax.broadcasted_iota(jnp.int32, shape, 2)


def shift(v, direction, amount):
    if direction == 1:
        return pltpu.roll(v, (-amount) % v.shape[1], 1)
    at = lane(v.shape)
    if direction == 2:
        r = pltpu.roll(v, (-amount * Z) % HALF, 2)
        other = jnp.stack([r[1], r[0]])
        stays = at < HALF - Z if amount > 0 else at >= Z
        return jnp.where(stays, r, other)
    near = pltpu.roll(v, (-amount) % HALF, 2)
    wrap = pltpu.roll(v, (amount * (Z - 1)) % HALF, 2)
    z = at % Z
    stays = z < Z - 1 if amount > 0 else z > 0
    return jnp.where(stays, near, wrap)


def split(row):
    return jnp.stack([row[:, :HALF], row[:, HALF:]])


def sin_cos(turns):
    r = turns - jnp.round(turns)
    u = r * r
    s = SIN[-1]
    for a in SIN[-2::-1]:
        s = s * u + a
    c = COS[-1]
    for a in COS[-2::-1]:
        c = c * u + a
    return s * r, c


def curl(here, ahead, plane):
    m, k = plane
    moved = ahead[k] if m == 0 else shift(here[k], m, 1)
    return (here[m] - shift(here[m], k, 1)) + (moved - here[k])


def stage(size, read, weights, scratch, write, read_v=None, sums=None):
    square, oblong = weights
    sin, cos, vec, force, edge = scratch

    def plaquettes(t, carry):
        here = [read(d, t) for d in range(4)]
        ahead = [read(d, t + 1) for d in range(4)]
        for j, plane in enumerate(PLANES):
            s, c = sin_cos(curl(here, ahead, plane))
            sin[j, t] = s
            cos[j, t] = c
        if read_v is not None:
            here = [read_v(d, t) for d in range(4)]
            ahead = [read_v(d, t + 1) for d in range(4)]
            for j, plane in enumerate(PLANES):
                vec[j, t] = curl(here, ahead, plane)
        return carry

    lax.fori_loop(0, size - 1, plaquettes, 0)

    def pair(j, direction, t, row):
        s, c, q = row
        if direction == 0:
            s2, c2 = sin[j, t + 1], cos[j, t + 1]
        else:
            s2, c2 = shift(s, direction, 1), shift(c, direction, 1)
        if read_v is None:
            return s * c2 + c * s2, None
        q2 = vec[j, t + 1] if direction == 0 else shift(q, direction, 1)
        both = q + q2
        return (c * c2 - s * s2) * both, (s * c2 + c * s2, both)

    def load(j, t):
        return sin[j, t], cos[j, t], None if read_v is None else vec[j, t]

    for j in range(3):
        edge[j, 0] = pair(j, 0, 0, load(j, 0))[0]

    def forces(t, carry, summed):
        for j, (m, k) in enumerate(PLANES):
            row = load(j, t)
            s, c, q = row
            total = square[j] * (s if read_v is None else c * q)
            if summed:
                sums[2](j, s * q)
            for direction, other in ((m, k), (k, m)):
                value, term = pair(j, direction, t, row)
                if summed:
                    sums[2](6 + oblong_index(direction, other), term[0] * term[1])
                if direction == 0:
                    edge[j, t] = value
                    back = edge[j, t - 1]
                else:
                    back = shift(value, direction, -1)
                total = total + oblong[oblong_index(direction, other)] * (value + back)
            force[j, t] = total
        return carry

    if sums is None:
        lax.fori_loop(1, size - 2, lambda t, a: forces(t, a, False), 0)
    else:
        lax.fori_loop(1, sums[0], lambda t, a: forces(t, a, False), 0)
        lax.fori_loop(sums[0], sums[1], lambda t, a: forces(t, a, True), 0)
        lax.fori_loop(sums[1], size - 2, lambda t, a: forces(t, a, False), 0)

    def links(t, carry):
        parts = [None] * 4
        for j, (m, k) in enumerate(PLANES):
            h = force[j, t]
            back_k = shift(h, k, -1)
            back_m = force[j, t - 1] if m == 0 else shift(h, m, -1)
            first, second = back_k - h, h - back_m
            parts[m] = first if parts[m] is None else parts[m] + first
            parts[k] = second if parts[k] is None else parts[k] + second
        write(t, parts)
        return carry

    lax.fori_loop(2, size - 2, links, 0)


WIDE = 3 * BLOCK
NARROW = 2 * BLOCK
WIDE_X = 16


def stage_scratch():
    rows = [6, 6, 6, 6, 3]
    return [pltpu.VMEM((n, WIDE, 2, WIDE_X, HALF), F32) for n in rows] + [
        pltpu.VMEM((n, NARROW, 2, NARROW, HALF), F32) for n in rows
    ]


def assemble(core, block, mine, theirs, wide):
    def fill(left, right):
        b = BLOCK
        wide[:, b:2 * b, b:2 * b, :] = block[...]
        for ref, rows, columns in ((left, (0, 1, 0, 2), (1, 0, 0, 0)), (right, (2, 1, 2, 0), (1, 2, 2, 2))):
            for i, (r, c) in enumerate(zip(rows, columns)):
                wide[:, r * b:(r + 1) * b, c * b:(c + 1) * b, :] = ref[:, i * b:(i + 1) * b]

    wide[:, :, WIDE:, :] = jnp.zeros(wide.shape[:2] + (WIDE_X - WIDE, 2 * HALF), F32)

    @pl.when(core == 0)
    def _():
        fill(mine, theirs)

    @pl.when(core != 0)
    def _():
        fill(theirs, mine)


def wide_row(wide, first=0):
    return lambda d, t: split(wide[first + d, t])


def wide_crop(wide, d, t):
    return inner(split(wide[d, t + 2]), NARROW)


def inner(row, count):
    return pltpu.roll(row, row.shape[1] - 2, 1)[:, :count]


def narrow_row(ref):
    return lambda d, t: ref[d, t]


def put_block(out, d, t, row):
    out[d, t, :, :HALF] = row[0]
    out[d, t, :, HALF:] = row[1]


def row_weights(square, oblong, step):
    return [square[step, j] for j in range(6)], [oblong[step, j] for j in range(12)]


def forward_kernel(kind, steps, core, square, oblong, block, mine, theirs, *rest):
    if kind == 0:
        narrow, out, wide, drift, *scratch = rest
        previous = None
    else:
        previous, narrow, out, wide, drift, *scratch = rest
    assemble(core[0], block, mine, theirs, wide)
    unit = STEP / TURN

    def write_wide(t, parts):
        for d in range(4):
            z = inner(parts[d], NARROW) * unit
            at = t - 2
            if kind == 0:
                drift[d, at] = z
                narrow[d, at] = wide_crop(wide, d, at) + 0.25 * z
            elif kind == 1:
                narrow[d, at] = previous[d, at] + 0.75 * z
            else:
                second = wide_crop(wide, d, at)
                narrow[d, at] = second + 8.0 / 9.0 * z - 17.0 / 9.0 * (second - previous[d, at])

    stage(WIDE, wide_row(wide), row_weights(square, oblong, steps[0]), scratch[:5], write_wide)

    def write_narrow(t, parts):
        for d in range(4):
            z = parts[d] * unit
            if kind == 0:
                value = narrow[d, t] + 8.0 / 9.0 * z - 17.0 / 36.0 * drift[d, t]
            elif kind == 1:
                value = narrow[d, t] + 0.25 * z
            else:
                value = wide_crop(wide, d, t) + 0.75 * z
            put_block(out, d, t - 2, inner(value, BLOCK))

    stage(NARROW, narrow_row(narrow), row_weights(square, oblong, steps[1]), scratch[5:], write_narrow)


def summing(total, first, width):
    def accumulate(index, value):
        total[index] += value[:, :8]
    total[...] = jnp.zeros(total.shape, F32)

    def finish(out, place, factor=1.0):
        at = lax.broadcasted_iota(jnp.int32, (1, 8, HALF), 1)
        kept = (at >= first) & (at < first + BLOCK)
        for index in range(18):
            value = jnp.where(kept, total[index], 0.0)
            value = jnp.sum(value, 0) * factor
            out[place, index:index + 1, :] = jnp.sum(value, 0, keepdims=True)
    return accumulate, finish


def backward_kernel(kind, steps, core, square, oblong, block, mine, theirs, *rest):
    fields = block.shape[0]
    base_wide = None
    rest = list(rest)
    if fields == 4:
        base_wide = rest.pop(0)
    base_narrow = rest.pop(0)
    known = [rest.pop(0) for _ in range(min(kind, 1))]
    narrow, out, out_two, sums_out, wide, keep, total, *scratch = rest
    assemble(core[0], block, mine, theirs, wide)
    if base_wide is None:
        base = wide_row(wide)
        vector = wide_row(wide, 4)
        crop = lambda d, t: wide_crop(wide, 4 + d, t)
    else:
        base = wide_row(base_wide)
        vector = wide_row(wide)
        crop = lambda d, t: wide_crop(wide, d, t)
    factor = (0.75, 1.0, 8.0 / 9.0)[kind]

    def write_wide(t, parts):
        at = t - 2
        for d in range(4):
            image = inner(parts[d], NARROW) * (STEP * factor)
            here = crop(d, at)
            if kind == 0:
                narrow[d, at] = image
                keep[d, at] = here + image
            elif kind == 1:
                narrow[d, at] = 4.0 * here + 17.0 / 9.0 * known[0][d, at] + image
            else:
                after = known[0][d, at] + here + image
                keep[d, at] = after
                narrow[d, at] = 0.25 * after - 17.0 / 36.0 * here

    accumulate, finish = summing(total, BLOCK, WIDE)
    stage(WIDE, base, row_weights(square, oblong, steps[0]), scratch[:5], write_wide,
          read_v=vector, sums=(BLOCK, 2 * BLOCK, accumulate))
    finish(sums_out, 0, factor)
    factor_two = (8.0 / 9.0, 0.75, 1.0)[kind]

    def write_narrow(t, parts):
        for d in range(4):
            image = parts[d] * (STEP * factor_two)
            if kind == 0:
                after = keep[d, t] + image
                value = 0.25 * after - 17.0 / 36.0 * narrow[d, t]
                put_block(out_two, d, t - 2, inner(after, BLOCK))
            elif kind == 1:
                value = image
            else:
                value = keep[d, t] + image
            put_block(out, d, t - 2, inner(value, BLOCK))

    accumulate, finish = summing(total, 2, NARROW)
    stage(NARROW, narrow_row(base_narrow), row_weights(square, oblong, steps[1]), scratch[5:], write_narrow,
          read_v=narrow_row(narrow), sums=(2, 2 + BLOCK, accumulate))
    finish(sums_out, 1, factor_two)


def last_kernel(core, square, oblong, block, mine, theirs, base_wide, after, out, sums_out, wide, vec, base, total, *scratch):
    assemble(core[0], block, mine, theirs, wide)

    def crop(t, carry):
        for d in range(4):
            vec[d, t] = wide_crop(wide, d, t)
            base[d, t] = wide_crop(base_wide, d, t)
        return carry

    lax.fori_loop(0, NARROW, crop, 0)

    def write(t, parts):
        for d in range(4):
            row = inner(parts[d], BLOCK) * STEP
            out[d, t - 2, :, :HALF] = after[d, t - 2, :, :HALF] + row[0]
            out[d, t - 2, :, HALF:] = after[d, t - 2, :, HALF:] + row[1]

    accumulate, finish = summing(total, 2, NARROW)
    stage(NARROW, narrow_row(base), row_weights(square, oblong, 0), scratch[5:], write,
          read_v=narrow_row(vec), sums=(2, 2 + BLOCK, accumulate))
    finish(sums_out, 0)


VMEM = pl.BlockSpec(memory_space=pltpu.VMEM)
SMEM = pl.BlockSpec(memory_space=pltpu.SMEM)
NARROW_SHAPE = jax.ShapeDtypeStruct((4, NARROW, 2, NARROW, HALF), F32)
BLOCK_SHAPE = jax.ShapeDtypeStruct((4, BLOCK, BLOCK, 2 * HALF), F32)
WIDE_SHAPE = jax.ShapeDtypeStruct((4, WIDE, WIDE_X, 2 * HALF), F32)


def scratch_of(shape):
    return pltpu.VMEM(shape.shape, F32)


def call(kernel, out_shape, scratch, scalars, arrays):
    return pl.pallas_call(
        kernel,
        out_shape=out_shape,
        in_specs=[SMEM] * len(scalars) + [VMEM] * len(arrays),
        out_specs=[VMEM] * len(out_shape),
        scratch_shapes=scratch + stage_scratch(),
        compiler_params=pltpu.CompilerParams(vmem_limit_bytes=40 * 2**20),
    )(*scalars, *arrays)


def forward(kind, steps, scalars, block, previous=None):
    def kernel(core, square, oblong, block, mine, theirs, *rest):
        if kind == 0:
            wide, narrow, out, drift, *scratch = rest
            rest = (narrow, out, wide, drift, *scratch)
        else:
            previous, wide, narrow, out, drift, *scratch = rest
            rest = (previous, narrow, out, wide, drift, *scratch)
        forward_kernel(kind, steps, core, square, oblong, block, mine, theirs, *rest)

    arrays = [block, *exchange(block)] + ([] if previous is None else [previous])
    return call(kernel, [WIDE_SHAPE, NARROW_SHAPE, BLOCK_SHAPE], [scratch_of(NARROW_SHAPE)], scalars, arrays)


def backward(kind, steps, scalars, block, bases, known):
    fields = block.shape[0]

    def kernel(core, square, oblong, *rest):
        backward_kernel(kind, steps, core, square, oblong, *rest)

    wide = pltpu.VMEM((fields,) + WIDE_SHAPE.shape[1:], F32)
    scratch = [wide, scratch_of(NARROW_SHAPE), pltpu.VMEM((18, 2, 8, HALF), F32)]
    sums = jax.ShapeDtypeStruct((2, 18, HALF), F32)
    shapes = [NARROW_SHAPE, BLOCK_SHAPE, BLOCK_SHAPE, sums]
    return call(kernel, shapes, scratch, scalars, [block, *exchange(block), *bases, *known])


def last(scalars, block, base_wide, after):
    scratch = [scratch_of(WIDE_SHAPE), scratch_of(NARROW_SHAPE), scratch_of(NARROW_SHAPE),
               pltpu.VMEM((18, 2, 8, HALF), F32)]
    sums = jax.ShapeDtypeStruct((1, 18, HALF), F32)
    return call(last_kernel, [BLOCK_SHAPE, sums], scratch, scalars, [block, *exchange(block), base_wide, after])


def on_device(link_angles, cotangent, square_weight, oblong_weight):
    core = lax.axis_index("ta") % 2
    scalars = (core.reshape(1).astype(jnp.int32), square_weight, oblong_weight)
    own = jnp.concatenate([link_angles * (1.0 / TURN), cotangent], 0)
    own = permute(own, lambda t, x, c: (t, x, c), home, place)
    other = swap_cores(own)
    chip = jnp.concatenate([jnp.where(core == 0, own, other), jnp.where(core == 0, other, own)], 1)

    w0, w1, b2 = forward(0, (0, 0), scalars, chip[:4])
    w2, w3, b4 = forward(1, (0, 1), scalars, b2, w1)
    w4, w5, b6 = forward(2, (1, 1), scalars, b4, w3)
    w6, w7, b8 = forward(0, (2, 2), scalars, b6)

    image, grad, _, sums_8 = backward(0, (2, 2), scalars, jnp.concatenate([b8, chip[4:]], 0), (w7,), ())
    before, image, _, sums_6 = backward(1, (2, 1), scalars, grad, (w6, w5), (image,))
    _, adjoint, _, sums_4 = backward_two(scalars, image, (w4, w3), before)
    _, grad, after, sums_2 = backward(0, (0, 0), scalars, adjoint, (w2, w1), ())
    result, sums_0 = last(scalars, grad, w0, after)

    result = lax.dynamic_slice_in_dim(result, 2 * core, 2, 1)
    result = permute(result, lambda t, x, c: (t, x, c), place, home)

    steps = [sums_2[0] + sums_2[1] + sums_0[0], sums_6[1] + sums_4[0] + sums_4[1], sums_8[0] + sums_8[1] + sums_6[0]]
    rows = jnp.sum(jnp.stack(steps), 2).reshape(54) * (-0.5 * STEP)
    rows = jnp.broadcast_to(jnp.pad(rows, (0, HALF - 54))[None], (256, HALF))
    rows = lax.all_to_all(rows, ("ta", "gx"), 0, 0, tiled=True)
    sites = 16 * 8 * BLOCK * BLOCK * 2 * HALF
    totals = (jnp.sum(rows, 0)[:54] * (1.0 / math.sqrt(sites))).reshape(STEPS, 18)
    return result, totals[:, :6], totals[:, 6:]


def backward_two(scalars, image, bases, before):
    return backward(2, (1, 1), scalars, image, bases, (before,))


def solution(mesh):
    in_specs = (P(None, "ta", "gx", None), P(None, "ta", "gx", None), P(), P())
    out_specs = (P(None, "ta", "gx", None), P(), P())
    return jax.shard_map(on_device, mesh=mesh, in_specs=in_specs, out_specs=out_specs, check_vma=False)
```

```python
import functools
import math

import jax
import jax.numpy as jnp
import numpy as np
from jax import lax
from jax.experimental import pallas as pl
from jax.experimental.pallas import tpu as pltpu
from jax.sharding import PartitionSpec as P


Z = 16
STEPS = 3
STEP = 0.05
TURN = 2.0 * math.pi
PLANES = [(0, 1), (0, 2), (0, 3), (1, 2), (1, 3), (2, 3)]
BLOCK = 4
HALF = 128
F32 = jnp.float32

SIN = [6.283182621002197, -41.34142303466797, 81.59618377685547,
       -76.5801010131836, 41.20539093017578, -12.271258354187012]
COS = [1.0, -19.73920440673828, 64.93911743164062, -85.45016479492188,
       60.16783142089844, -25.968311309814453, 6.529608726501465]


def oblong_index(first, second):
    return first * 3 + second - int(second > first)


def home(tau, xi, core):
    return ((tau % 16) * 2 + core) * 8 + xi % 8


def place(tau, xi, core):
    p = (tau + 12) % 16
    z, y_hi = (p, 0) if p < 8 else (15 - p, 1)
    xi = xi % 8
    x, side = (xi, 0) if xi < 4 else (7 - xi, 1)
    y_lo = side if y_hi == 0 else 1 - side
    return (z * 4 + y_hi * 2 + core) * 8 + y_lo * 4 + x


EVERY = [(t, x, c) for t in range(16) for x in range(8) for c in range(2)]


def permute(array, source, start=place, end=place):
    pairs = [(start(*source(t, x, c)), end(t, x, c)) for t, x, c in EVERY]
    return lax.ppermute(array, ("ta", "gx"), pairs)


def swap_cores(array):
    return permute(array, lambda t, x, c: (t, x, 1 - c))


SOURCES = [((-1, 0), (1, 0)), ((0, -1), (0, 1)), ((-1, -1), (1, 1)), ((1, -1), (-1, 1))]


def exchange(block):
    parts = []
    for choices in SOURCES:
        def source(t, x, c, choices=choices):
            return (t + choices[c][0], x + choices[c][1], 1 - c)
        parts.append(permute(block, source))
    mine = jnp.concatenate(parts, 1)
    return mine, swap_cores(mine)


def lane_order():
    return [(2 * yy + h) * Z + z for h in range(2) for z in range(Z) for yy in range(8)]


def relabel(array, back=False):
    matrix = np.zeros((2 * HALF, 2 * HALF), np.float32)
    matrix[lane_order(), np.arange(2 * HALF)] = 1.0
    if back:
        matrix = matrix.T
    flat = array.reshape(-1, 2 * HALF)
    flat = lax.dot(flat, jnp.asarray(matrix), precision=lax.Precision.HIGHEST, preferred_element_type=F32)
    return flat.reshape(array.shape)


def roll(v, amount, axis):
    axis = axis % v.ndim
    return pltpu.roll(v, amount % v.shape[axis], axis)


def step_y(v, amount):
    yy = lax.broadcasted_iota(jnp.int32, v.shape, v.ndim - 1) % 8
    stays = yy < 7 if amount > 0 else yy > 0
    return jnp.where(stays, roll(v, -amount, -1), roll(v, 7 * amount, -1))


def shift(v, direction, amount):
    if direction == 1:
        return roll(v, -amount, -2)
    if direction == 3:
        return roll(v, -8 * amount, -1)
    even, odd = v[:, 0], v[:, 1]
    if amount > 0:
        return jnp.stack([odd, step_y(even, 1)], 1)
    return jnp.stack([step_y(odd, -1), even], 1)


def sin_cos(turns):
    r = turns - jnp.round(turns)
    u = r * r
    s = SIN[-1]
    for a in SIN[-2::-1]:
        s = s * u + a
    c = COS[-1]
    for a in COS[-2::-1]:
        c = c * u + a
    return s * r, c


def curl(here, ahead, plane):
    m, k = plane
    moved = ahead[k] if m == 0 else shift(here[k], m, 1)
    return (here[m] - shift(here[m], k, 1)) + (moved - here[k])


def loop(first, last, n, body):
    count = (last - first) // n

    def run(i, carry):
        body(first + n * i, n)
        return carry

    if count:
        lax.fori_loop(0, count, run, 0)
    if (last - first) % n:
        body(first + n * count, (last - first) % n)


def inner(rows, count):
    return roll(rows, -2, -2)[..., :count, :]


def at(ref, index, t, n):
    return ref[index, pl.ds(t, n)]


def directions(j):
    m, k = PLANES[j]
    return [(m, oblong_index(m, k)), (k, oblong_index(k, m))]


def add_back(total, value, j, direction, edge, weight):
    if direction == 0:
        back = jnp.concatenate([edge[j][None], value[:-1]], 0)
        edge[j] = value[-1]
    else:
        back = shift(value, direction, -1)
    return total + weight * (value + back)


def base_pass(size, own, read, weights, sin, cos, cosines, sines, force=None, edge=None):
    square, oblong = weights

    def plaquettes(t, n):
        here = [read(d, t, n) for d in range(4)]
        ahead = [read(d, t + 1, n) for d in range(4)]
        for j, plane in enumerate(PLANES):
            s, c = sin_cos(curl(here, ahead, plane))
            sin[j, pl.ds(t, n)] = s
            cos[j, pl.ds(t, n)] = c

    loop(0, size - 1, 1, plaquettes)

    def forces(is_own, t, n):
        for j in range(6):
            s, c = at(sin, j, t, n), at(cos, j, t, n)
            if force is not None:
                total = square[j] * s
            if is_own:
                sines[j, pl.ds(t - own, n)] = s[:, :, :8]
            for direction, index in directions(j):
                if direction == 0:
                    s2, c2 = at(sin, j, t + 1, n), at(cos, j, t + 1, n)
                else:
                    s2, c2 = shift(s, direction, 1), shift(c, direction, 1)
                cosines[index, pl.ds(t, n)] = c * c2 - s * s2
                if is_own or force is not None:
                    value = s * c2 + c * s2
                if is_own:
                    sines[6 + index, pl.ds(t - own, n)] = value[:, :, :8]
                if force is not None:
                    total = add_back(total, value, j, direction, edge, oblong[index])
            if force is not None:
                force[j, pl.ds(t, n)] = total

    loop(0, own, 2, functools.partial(forces, False))
    loop(own, own + BLOCK, 2, functools.partial(forces, True))
    loop(own + BLOCK, size - 2, 2, functools.partial(forces, False))


def vector_pass(size, own, read, weights, cos_at, cosines_at, sines_at, vec, force, edge, total):
    square, oblong = weights

    def plaquettes(t, n):
        here = [read(d, t, n) for d in range(4)]
        ahead = [read(d, t + 1, n) for d in range(4)]
        for j, plane in enumerate(PLANES):
            vec[j, pl.ds(t, n)] = curl(here, ahead, plane)

    loop(0, size - 1, 2, plaquettes)
    total[...] = jnp.zeros(total.shape, F32)

    def forces(is_own, t, n):
        for j in range(6):
            q = at(vec, j, t, n)
            result = square[j] * (cos_at(j, t, n) * q)
            if is_own:
                total[j] += jnp.sum(sines_at(j, t - own, n) * q[:, :, :8], 0)
            for direction, index in directions(j):
                both = q + (at(vec, j, t + 1, n) if direction == 0 else shift(q, direction, 1))
                if is_own:
                    total[6 + index] += jnp.sum(sines_at(6 + index, t - own, n) * both[:, :, :8], 0)
                value = cosines_at(index, t, n) * both
                result = add_back(result, value, j, direction, edge, oblong[index])
            force[j, pl.ds(t, n)] = result

    loop(0, own, 2, functools.partial(forces, False))
    loop(own, own + BLOCK, 2, functools.partial(forces, True))
    loop(own + BLOCK, size - 2, 2, functools.partial(forces, False))


def link_pass(size, force, write):
    def links(t, n):
        parts = [None] * 4
        for j, (m, k) in enumerate(PLANES):
            h = at(force, j, t, n)
            back_m = at(force, j, t - 1, n) if m == 0 else shift(h, m, -1)
            first, second = shift(h, k, -1) - h, h - back_m
            parts[m] = first if parts[m] is None else parts[m] + first
            parts[k] = second if parts[k] is None else parts[k] + second
        write(t, n, parts)

    loop(2, size - 2, 2, links)


WIDE = 3 * BLOCK
NARROW = 2 * BLOCK
WIDE_X = 16


def region(fields, wide):
    rows, columns = (WIDE, WIDE_X) if wide else (NARROW, NARROW)
    return jax.ShapeDtypeStruct((fields, rows, 2, columns, HALF), F32)


def edge_region(wide):
    return jax.ShapeDtypeStruct((3, 2, WIDE_X if wide else NARROW, HALF), F32)


BLOCK_SHAPE = jax.ShapeDtypeStruct((4, BLOCK, BLOCK, 2 * HALF), F32)
OWN_SHAPE = jax.ShapeDtypeStruct((18, BLOCK, 2, 8, HALF), F32)
SUMS_SHAPE = jax.ShapeDtypeStruct((18, 8, HALF), F32)
TOTAL_SHAPE = jax.ShapeDtypeStruct((18, 2, 8, HALF), F32)


def assemble(core, block, mine, theirs, wide):
    b = BLOCK

    def put(row, column, value):
        for h in range(2):
            wide[:, row * b:(row + 1) * b, h, column * b:(column + 1) * b, :] = value[..., h * HALF:(h + 1) * HALF]

    def fill(left, right):
        for ref, rows, columns in ((left, (0, 1, 0, 2), (1, 0, 0, 0)), (right, (2, 1, 2, 0), (1, 2, 2, 2))):
            for i, (row, column) in enumerate(zip(rows, columns)):
                put(row, column, ref[:, i * b:(i + 1) * b])

    put(1, 1, block[...])

    @pl.when(core == 0)
    def _():
        fill(mine, theirs)

    @pl.when(core != 0)
    def _():
        fill(theirs, mine)


def rows_of(ref, first=0):
    return lambda d, t, n: ref[first + d, pl.ds(t, n)]


def crop_of(ref, first=0):
    return lambda d, t, n: inner(ref[first + d, pl.ds(t + 2, n)], NARROW)


def put_block(out, d, t, n, rows):
    out[d, pl.ds(t, n), :, :HALF] = rows[:, 0]
    out[d, pl.ds(t, n), :, HALF:] = rows[:, 1]


def row_weights(square, oblong, step):
    return [square[step, j] for j in range(6)], [oblong[step, j] for j in range(12)]


def forward_kernel(kind, steps, core, square, oblong, block, mine, theirs, *rest):
    rest = list(rest)
    previous = rest.pop(0) if kind else None
    narrow, out, cos_w, cosines_w, sines_w, cos_n, cosines_n, sines_n = rest[:8]
    wide, drift, sin_w, force_w, edge_w, sin_n, force_n, edge_n = rest[8:]
    assemble(core[0], block, mine, theirs, wide)
    crop = crop_of(wide)
    unit = STEP / TURN

    def write_wide(t, n, parts):
        here = pl.ds(t - 2, n)
        for d in range(4):
            z = inner(parts[d], NARROW) * unit
            if kind == 0:
                drift[d, here] = z
                narrow[d, here] = crop(d, t - 2, n) + 0.25 * z
            elif kind == 1:
                narrow[d, here] = previous[d, here] + 0.75 * z
            else:
                second = crop(d, t - 2, n)
                narrow[d, here] = second + 8.0 / 9.0 * z - 17.0 / 9.0 * (second - previous[d, here])

    base_pass(WIDE, BLOCK, rows_of(wide), row_weights(square, oblong, steps[0]),
              sin_w, cos_w, cosines_w, sines_w, force_w, edge_w)
    link_pass(WIDE, force_w, write_wide)

    def write_narrow(t, n, parts):
        here = pl.ds(t, n)
        for d in range(4):
            z = parts[d] * unit
            if kind == 0:
                value = narrow[d, here] + 8.0 / 9.0 * z - 17.0 / 36.0 * drift[d, here]
            elif kind == 1:
                value = narrow[d, here] + 0.25 * z
            else:
                value = crop(d, t, n) + 0.75 * z
            put_block(out, d, t - 2, n, inner(value, BLOCK))

    base_pass(NARROW, 2, rows_of(narrow), row_weights(square, oblong, steps[1]),
              sin_n, cos_n, cosines_n, sines_n, force_n, edge_n)
    link_pass(NARROW, force_n, write_narrow)


def put_sums(out, total, first, factor):
    x = lax.broadcasted_iota(jnp.int32, (8, HALF), 0)
    kept = (x >= first) & (x < first + BLOCK)
    for index in range(18):
        out[index] = jnp.where(kept, (total[index, 0] + total[index, 1]) * factor, 0.0)


def read_base(cos, cosines, sines):
    def reader(ref):
        return lambda index, t, n: at(ref, index, t, n)
    return reader(cos), reader(cosines), reader(sines)


def backward_kernel(kind, steps, core, square, oblong, block, mine, theirs, *rest):
    first = block.shape[0] - 4
    rest = list(rest)
    base_w = None if first else [rest.pop(0) for _ in range(3)]
    base_n = [rest.pop(0) for _ in range(3)]
    known = rest.pop(0) if kind else None
    narrow, out, out_two, sums_one, sums_two = rest[:5]
    wide, keep, total, vec_w, force_w, edge_w, vec_n, force_n, edge_n, *sin_w = rest[5:]
    assemble(core[0], block, mine, theirs, wide)
    weights = row_weights(square, oblong, steps[0])
    if first:
        sin_w, *base_w = sin_w
        base_pass(WIDE, BLOCK, rows_of(wide), weights, sin_w, *base_w)
    crop = crop_of(wide, first)
    factor = (0.75, 1.0, 8.0 / 9.0)[kind]

    def write_wide(t, n, parts):
        here = pl.ds(t - 2, n)
        for d in range(4):
            image = inner(parts[d], NARROW) * (STEP * factor)
            source = crop(d, t - 2, n)
            if kind == 0:
                narrow[d, here] = image
                keep[d, here] = source + image
            elif kind == 1:
                narrow[d, here] = 4.0 * source + 17.0 / 9.0 * known[d, here] + image
            else:
                after = known[d, here] + source + image
                keep[d, here] = after
                narrow[d, here] = 0.25 * after - 17.0 / 36.0 * source

    vector_pass(WIDE, BLOCK, rows_of(wide, first), weights, *read_base(*base_w), vec_w, force_w, edge_w, total)
    link_pass(WIDE, force_w, write_wide)
    put_sums(sums_one, total, BLOCK, factor)
    factor_two = (8.0 / 9.0, 0.75, 1.0)[kind]

    def write_narrow(t, n, parts):
        here = pl.ds(t, n)
        for d in range(4):
            image = parts[d] * (STEP * factor_two)
            if kind == 0:
                after = keep[d, here] + image
                value = 0.25 * after - 17.0 / 36.0 * narrow[d, here]
                put_block(out_two, d, t - 2, n, inner(after, BLOCK))
            elif kind == 1:
                value = image
            else:
                value = keep[d, here] + image
            put_block(out, d, t - 2, n, inner(value, BLOCK))

    vector_pass(NARROW, 2, rows_of(narrow), row_weights(square, oblong, steps[1]), *read_base(*base_n),
                vec_n, force_n, edge_n, total)
    link_pass(NARROW, force_n, write_narrow)
    put_sums(sums_two, total, 2, factor_two)


def last_kernel(core, square, oblong, block, mine, theirs, cos, cosines, sines, after, out, sums,
                wide, total, vec, force, edge):
    assemble(core[0], block, mine, theirs, wide)

    def sines_at(index, t, n):
        return roll(at(sines, index, t, n), -2, -2)

    def write(t, n, parts):
        for d in range(4):
            image = inner(parts[d], BLOCK) * STEP
            here = after[d, pl.ds(t - 2, n)]
            put_block(out, d, t - 2, n, jnp.stack([here[..., :HALF], here[..., HALF:]], 1) + image)

    vector_pass(NARROW, 2, crop_of(wide), row_weights(square, oblong, 0), crop_of(cos), crop_of(cosines), sines_at,
                vec, force, edge, total)
    link_pass(NARROW, force, write)
    put_sums(sums, total, 2, 1.0)


VMEM = pl.BlockSpec(memory_space=pltpu.VMEM)
SMEM = pl.BlockSpec(memory_space=pltpu.SMEM)


def call(kernel, outs, scratch, scalars, arrays):
    return pl.pallas_call(
        kernel,
        out_shape=outs,
        in_specs=[SMEM] * len(scalars) + [VMEM] * len(arrays),
        out_specs=[VMEM] * len(outs),
        scratch_shapes=[pltpu.VMEM(shape.shape, F32) for shape in scratch],
        compiler_params=pltpu.CompilerParams(vmem_limit_bytes=24 * 2**20),
    )(*scalars, *arrays)


def base_shapes(wide):
    return [region(6, wide), region(12, wide), OWN_SHAPE]


def forward(kind, steps, scalars, block, previous=None):
    arrays = [block, *exchange(block)] + ([] if previous is None else [previous])
    outs = [region(4, False), BLOCK_SHAPE, *base_shapes(True), *base_shapes(False)]
    scratch = [region(4, True), region(4, False)]
    for wide in (True, False):
        scratch += [region(6, wide), region(6, wide), edge_region(wide)]
    kernel = functools.partial(forward_kernel, kind, steps)
    narrow, out, *bases = call(kernel, outs, scratch, scalars, arrays)
    return narrow, out, bases[:3], bases[3:]


def backward(kind, steps, scalars, block, bases, known=None):
    fields = block.shape[0]
    arrays = [block, *exchange(block)] + [array for base in bases for array in base]
    arrays += [] if known is None else [known]
    outs = [region(4, False), BLOCK_SHAPE, BLOCK_SHAPE, SUMS_SHAPE, SUMS_SHAPE]
    scratch = [region(fields, True), region(4, False), TOTAL_SHAPE]
    for wide in (True, False):
        scratch += [region(6, wide), region(6, wide), edge_region(wide)]
    if fields == 8:
        scratch += [region(6, True), *base_shapes(True)]
    return call(functools.partial(backward_kernel, kind, steps), outs, scratch, scalars, arrays)


def last(scalars, block, base, after):
    scratch = [region(4, True), TOTAL_SHAPE, region(6, False), region(6, False), edge_region(False)]
    arrays = [block, *exchange(block), *base, after]
    return call(last_kernel, [BLOCK_SHAPE, SUMS_SHAPE], scratch, scalars, arrays)


def on_device(link_angles, cotangent, square_weight, oblong_weight):
    core = lax.axis_index("ta") % 2
    scalars = (core.reshape(1).astype(jnp.int32), square_weight, oblong_weight)
    own = relabel(jnp.concatenate([link_angles * (1.0 / TURN), cotangent], 0))
    own = permute(own, lambda t, x, c: (t, x, c), home, place)
    other = swap_cores(own)
    chip = jnp.concatenate([jnp.where(core == 0, own, other), jnp.where(core == 0, other, own)], 1)

    w1, b2, base_0, base_1 = forward(0, (0, 0), scalars, chip[:4])
    w3, b4, base_2, base_3 = forward(1, (0, 1), scalars, b2, w1)
    w5, b6, base_4, base_5 = forward(2, (1, 1), scalars, b4, w3)
    w7, b8, base_6, base_7 = forward(0, (2, 2), scalars, b6)

    image, grad, _, sums_8, sums_7 = backward(0, (2, 2), scalars, jnp.concatenate([b8, chip[4:]], 0), (base_7,))
    before, image, _, sums_6, sums_5 = backward(1, (2, 1), scalars, grad, (base_6, base_5), image)
    _, adjoint, _, sums_4, sums_3 = backward(2, (1, 1), scalars, image, (base_4, base_3), before)
    _, grad, after, sums_2, sums_1 = backward(0, (0, 0), scalars, adjoint, (base_2, base_1))
    result, sums_0 = last(scalars, grad, base_0, after)

    result = lax.dynamic_slice_in_dim(result, 2 * core, 2, 1)
    result = relabel(permute(result, lambda t, x, c: (t, x, c), place, home), back=True)

    steps = [sums_0 + sums_1 + sums_2, sums_3 + sums_4 + sums_5, sums_6 + sums_7 + sums_8]
    rows = jnp.sum(jnp.stack(steps), (2, 3)).reshape(54) * (-0.5 * STEP)
    rows = jnp.broadcast_to(jnp.pad(rows, (0, HALF - 54))[None], (256, HALF))
    rows = lax.all_to_all(rows, ("ta", "gx"), 0, 0, tiled=True)
    sites = 16 * 8 * BLOCK * BLOCK * 2 * HALF
    totals = (jnp.sum(rows, 0)[:54] * (1.0 / math.sqrt(sites))).reshape(STEPS, 18)
    return result, totals[:, :6], totals[:, 6:]


def solution(mesh):
    in_specs = (P(None, "ta", "gx", None), P(None, "ta", "gx", None), P(), P())
    out_specs = (P(None, "ta", "gx", None), P(), P())
    return jax.shard_map(on_device, mesh=mesh, in_specs=in_specs, out_specs=out_specs, check_vma=False)
```

```python
import functools
import math

import jax
import jax.numpy as jnp
from jax import lax
from jax.experimental import pallas as pl
from jax.experimental.pallas import tpu as pltpu
from jax.sharding import PartitionSpec as P


Z = 16
STEPS = 3
STEP = 0.05
TURN = 2.0 * math.pi
PLANES = [(0, 1), (0, 2), (0, 3), (1, 2), (1, 3), (2, 3)]
BLOCK = 4
HALF = 128
F32 = jnp.float32

SIN = [4.442883014678955, -7.308241367340088, 3.6062889099121094, -0.8457635641098022, 0.10920574516057968]
COS = [1.4142135381698608, -6.978850841522217, 5.7394609451293945, -1.8835629224777222, 0.31069815158843994]


def oblong_index(first, second):
    return 6 + first * 3 + second - int(second > first)


def home(tau, xi, core):
    return ((tau % 16) * 2 + core) * 8 + xi % 8


def place(tau, xi, core):
    p = (tau + 12) % 16
    z, y_hi = (p, 0) if p < 8 else (15 - p, 1)
    xi = xi % 8
    x, side = (xi, 0) if xi < 4 else (7 - xi, 1)
    y_lo = side if y_hi == 0 else 1 - side
    return (z * 4 + y_hi * 2 + core) * 8 + y_lo * 4 + x


EVERY = [(t, x, c) for t in range(16) for x in range(8) for c in range(2)]


def permute(array, source, start=place, end=place):
    pairs = [(start(*source(t, x, c)), end(t, x, c)) for t, x, c in EVERY]
    return lax.ppermute(array, ("ta", "gx"), pairs)


def swap_cores(array):
    return permute(array, lambda t, x, c: (t, x, 1 - c))


SOURCES = [((-1, 0), (1, 0)), ((0, -1), (0, 1)), ((-1, -1), (1, 1)), ((1, -1), (-1, 1))]


def exchange(block):
    mine = []
    for choices in SOURCES:
        def source(t, x, c, choices=choices):
            return (t + choices[c][0], x + choices[c][1], 1 - c)
        mine.append(permute(block, source))
    return [block, *mine, *[swap_cores(part) for part in mine]]


WIDE = 3


def roll(v, amount, axis):
    axis = axis % v.ndim
    return pltpu.roll(v, amount % v.shape[axis], axis)


def sublane(v):
    return lax.broadcasted_iota(jnp.int32, v.shape, v.ndim - 2)


def step_t(one, two):
    tiles = [one[1:2], two[0:1]]
    if one.shape[0] == WIDE:
        a, b = one[2:], two[2:]
        tiles.append(roll(jnp.where(sublane(a) < 4, b, a), 4, -2))
    return jnp.concatenate(tiles, 0)


def step_x(v, amount):
    if v.shape[0] != WIDE:
        return roll(v, -amount, -2)
    even, odd, rest = v[0:1], v[1:2], v[2:]
    at = sublane(rest)
    if amount > 0:
        moved = roll(rest, -1, -2)
        return jnp.concatenate([
            jnp.where(at == 7, moved, roll(even, -1, -2)),
            jnp.where(at == 7, roll(rest, 3, -2), roll(odd, -1, -2)),
            moved], 0)
    moved = roll(even, 1, -2)
    last = jnp.where(at == 4, roll(odd, -3, -2), roll(rest, 1, -2))
    return jnp.concatenate([moved, roll(odd, 1, -2), jnp.where(at == 0, moved, last)], 0)


def step_y(v, amount):
    yy = lax.broadcasted_iota(jnp.int32, v.shape, v.ndim - 1) % 8
    stays = yy < 7 if amount > 0 else yy > 0
    return jnp.where(stays, roll(v, -amount, -1), roll(v, 7 * amount, -1))


def shift(v, direction, amount):
    if direction == 1:
        return step_x(v, amount)
    if direction == 3:
        return roll(v, -8 * amount, -1)
    even, odd = v[:, 0], v[:, 1]
    if amount > 0:
        return jnp.stack([odd, step_y(even, 1)], 1)
    return jnp.stack([step_y(odd, -1), even], 1)


def narrowed(v):
    even, odd, rest = v[0:1], v[1:2], v[2:]
    inside = sublane(rest) < 6
    return jnp.concatenate([
        jnp.where(inside, roll(even, -2, -2), roll(rest, 6, -2)),
        jnp.where(inside, roll(odd, -2, -2), roll(rest, 2, -2))], 0)


def inner(v):
    return roll(v, -2, -2)[:, :, :BLOCK]


def sin_cos(turns):
    r = turns - jnp.round(turns)
    u = r * r
    s = SIN[-1]
    for a in SIN[-2::-1]:
        s = s * u + a
    c = COS[-1]
    for a in COS[-2::-1]:
        c = c * u + a
    s = s * r
    return s * c, 1.0 - s * s


def curls(here, ahead):
    for m, k in PLANES:
        moved = step_t(here[k], ahead[k]) if m == 0 else shift(here[k], m, 1)
        yield (here[m] - shift(here[m], k, 1)) + (moved - here[k])


def directions(j):
    m, k = PLANES[j]
    return [(m, oblong_index(m, k)), (k, oblong_index(k, m))]


def loop(first, last, body):
    def run(p, carry):
        body(p)
        return carry

    if last > first:
        lax.fori_loop(first, last, run, 0)


def add_back(total, value, j, direction, edge, weight):
    if direction == 0:
        back = step_t(edge[j], value)
        edge[j] = value
    else:
        back = shift(value, direction, -1)
    return total + weight * (value + back)


def base_pass(pairs, own, read, weights, sin, cos, cosines, sines, force=None, edge=None):
    def plaquettes(p):
        here = [read(d, p) for d in range(4)]
        ahead = [read(d, jnp.minimum(p + 1, pairs - 1)) for d in range(4)]
        for j, angle in enumerate(curls(here, ahead)):
            sin[j, p], cos[j, p] = sin_cos(angle)

    loop(0, pairs, plaquettes)

    def forces(is_own, p):
        for j in range(6):
            s, c = sin[j, p], cos[j, p]
            if force is not None:
                total = weights[j] * s
            if is_own:
                sines[j, p - own] = s[:2]
            for direction, index in directions(j):
                if direction == 0:
                    s2, c2 = step_t(s, sin[j, p + 1]), step_t(c, cos[j, p + 1])
                else:
                    s2, c2 = shift(s, direction, 1), shift(c, direction, 1)
                cosines[index - 6, p] = c * c2 - s * s2
                if is_own or force is not None:
                    value = s * c2 + c * s2
                if is_own:
                    sines[index, p - own] = value[:2]
                if force is not None:
                    total = add_back(total, value, j, direction, edge, weights[index])
            if force is not None:
                force[j, p] = total

    loop(0, own, functools.partial(forces, False))
    loop(own, own + 2, functools.partial(forces, True))
    loop(own + 2, pairs - 1, functools.partial(forces, False))


def vector_pass(pairs, own, read, weights, cos_at, cosines_at, sines_at, vec, force, edge, total):
    def plaquettes(p):
        here = [read(d, p) for d in range(4)]
        ahead = [read(d, jnp.minimum(p + 1, pairs - 1)) for d in range(4)]
        for j, value in enumerate(curls(here, ahead)):
            vec[j, p] = value

    loop(0, pairs, plaquettes)
    total[...] = jnp.zeros(total.shape, F32)

    def forces(is_own, p):
        for j in range(6):
            q = vec[j, p]
            result = weights[j] * (cos_at(j, p) * q)
            if is_own:
                total[j] += jnp.sum(sines_at(j, p - own) * q[:2], 0)
            for direction, index in directions(j):
                both = q + (step_t(q, vec[j, p + 1]) if direction == 0 else shift(q, direction, 1))
                if is_own:
                    total[index] += jnp.sum(sines_at(index, p - own) * both[:2], 0)
                value = cosines_at(index - 6, p) * both
                result = add_back(result, value, j, direction, edge, weights[index])
            force[j, p] = result

    loop(0, own, functools.partial(forces, False))
    loop(own, own + 2, functools.partial(forces, True))
    loop(own + 2, pairs - 1, functools.partial(forces, False))


def link_pass(pairs, force, write):
    def links(p):
        parts = [None] * 4
        for j, (m, k) in enumerate(PLANES):
            h = force[j, p]
            back_m = step_t(force[j, p - 1], h) if m == 0 else shift(h, m, -1)
            first, second = shift(h, k, -1) - h, h - back_m
            parts[m] = first if parts[m] is None else parts[m] + first
            parts[k] = second if parts[k] is None else parts[k] + second
        write(p, parts)

    loop(1, pairs - 1, links)


WIDE_PAIRS = 6
NARROW_PAIRS = 4


def region(fields, wide, cut=0):
    pairs, tiles = (WIDE_PAIRS, WIDE) if wide else (NARROW_PAIRS, 2)
    return jax.ShapeDtypeStruct((fields, pairs - cut, tiles, 2, 8, HALF), F32)


def edge_region(wide):
    return jax.ShapeDtypeStruct((3, WIDE if wide else 2, 2, 8, HALF), F32)


def array_of(*shape):
    return jax.ShapeDtypeStruct(shape, F32)


HOME_SHAPE = array_of(4, 2, BLOCK, 2 * HALF)
BLOCK_SHAPE = array_of(4, BLOCK, BLOCK, 2 * HALF)
OWN_SHAPE = array_of(18, 2, 2, 2, 8, HALF)
SUMS_SHAPE = array_of(18, 8, HALF)
TOTAL_SHAPE = array_of(18, 2, 8, HALF)


def relabelled(rows, back):
    old = lax.broadcasted_iota(jnp.int32, (2 * HALF, 2 * HALF), 1 if back else 0)
    new = lax.broadcasted_iota(jnp.int32, (2 * HALF, 2 * HALF), 0 if back else 1)
    y, z = 2 * (new % 8) + new // HALF, (new % HALF) // 8
    matrix = jnp.where(old == y * Z + z, 1.0, 0.0).astype(F32)
    return lax.dot(rows, matrix, precision=lax.Precision.HIGHEST, preferred_element_type=F32)


def first_kernel(links, cotangent, out, rows):
    for f in range(8):
        for t in range(2):
            value = links[f, t] * (1.0 / TURN) if f < 4 else cotangent[f - 4, t]
            rows[(2 * f + t) * BLOCK:(2 * f + t + 1) * BLOCK] = value
    rows[...] = relabelled(rows[...], False)
    for f in range(8):
        for t in range(2):
            out[f, t] = rows[(2 * f + t) * BLOCK:(2 * f + t + 1) * BLOCK]


def assemble(core, blocks, wide):
    def put(row, column, block):
        for i in range(BLOCK):
            odd = i % 2
            tile = odd if column < 2 else 2
            x = BLOCK * (column if column < 2 else odd)
            for h in range(2):
                part = block[:, i, :, h * HALF:(h + 1) * HALF]
                wide[:, 2 * row + i // 2, tile, h, x:x + BLOCK, :] = part

    def fill(left, right):
        for block, row, column in zip(left, (0, 1, 0, 2), (1, 0, 0, 0)):
            put(row, column, block)
        for block, row, column in zip(right, (2, 1, 2, 0), (1, 2, 2, 2)):
            put(row, column, block)

    put(1, 1, blocks[0])

    @pl.when(core == 0)
    def _():
        fill(blocks[1:5], blocks[5:])

    @pl.when(core != 0)
    def _():
        fill(blocks[5:], blocks[1:5])


def rows_of(ref, first=0):
    return lambda d, p: ref[first + d, p]


def crop_of(ref, first=0):
    return lambda d, p: narrowed(ref[first + d, p + 1])


def put_block(out, d, p, v):
    at = pl.ds(2 * p - 2, 2)
    v = inner(v)
    out[d, at, :, :HALF] = v[:, 0]
    out[d, at, :, HALF:] = v[:, 1]


def row_weights(weights, step):
    return [weights[step, j] for j in range(18)]


def forward_kernel(kind, steps, core, weights, *rest):
    blocks, rest = rest[:9], list(rest[9:])
    previous = rest.pop(0) if kind else None
    narrow, out, cos_w, cosines_w, sines_w, cos_n, cosines_n, sines_n = rest[:8]
    wide, drift, sin_w, force_w, edge_w, sin_n, force_n, edge_n = rest[8:]
    assemble(core[0], blocks, wide)
    crop = crop_of(wide)
    unit = STEP / TURN

    def write_wide(p, parts):
        q = p - 1
        for d in range(4):
            z = narrowed(parts[d]) * unit
            if kind == 0:
                drift[d, q] = z
                narrow[d, q] = crop(d, q) + 0.25 * z
            elif kind == 1:
                narrow[d, q] = previous[d, q] + 0.75 * z
            else:
                second = crop(d, q)
                narrow[d, q] = second + 8.0 / 9.0 * z - 17.0 / 9.0 * (second - previous[d, q])

    base_pass(WIDE_PAIRS, 2, rows_of(wide), row_weights(weights, steps[0]),
              sin_w, cos_w, cosines_w, sines_w, force_w, edge_w)
    link_pass(WIDE_PAIRS, force_w, write_wide)

    def write_narrow(p, parts):
        for d in range(4):
            z = parts[d] * unit
            if kind == 0:
                value = narrow[d, p] + 8.0 / 9.0 * z - 17.0 / 36.0 * drift[d, p]
            elif kind == 1:
                value = narrow[d, p] + 0.25 * z
            else:
                value = crop(d, p) + 0.75 * z
            put_block(out, d, p, value)

    base_pass(NARROW_PAIRS, 1, rows_of(narrow), row_weights(weights, steps[1]),
              sin_n, cos_n, cosines_n, sines_n, force_n, edge_n)
    link_pass(NARROW_PAIRS, force_n, write_narrow)


def put_sums(out, total, first, factor, add=False):
    x = lax.broadcasted_iota(jnp.int32, (8, HALF), 0)
    kept = (x >= first) & (x < first + BLOCK)
    for index in range(18):
        value = jnp.where(kept, (total[index, 0] + total[index, 1]) * factor, 0.0)
        out[index] = out[index] + value if add else value


def readers(base):
    return [rows_of(ref) for ref in base]


def backward_kernel(kind, steps, core, weights, *rest):
    blocks, rest = rest[:9], list(rest[9:])
    first = blocks[0].shape[0] - 4
    base_w = None if first else [rest.pop(0) for _ in range(3)]
    base_n = [rest.pop(0) for _ in range(3)]
    known = rest.pop(0) if kind else None
    narrow, out, after_out, sums, other_sums = [rest.pop(0) for _ in range(5)]
    wide, keep, total, vec_w, force_w, edge_w, vec_n, force_n, edge_n, *base_scratch = rest
    assemble(core[0], blocks, wide)
    row = row_weights(weights, steps[0])
    if first:
        sin_w, *base_w = base_scratch
        base_pass(WIDE_PAIRS, 2, rows_of(wide), row, sin_w, *base_w)
    crop = crop_of(wide, first)
    factor = (0.75, 1.0, 8.0 / 9.0)[kind]

    def write_wide(p, parts):
        q = p - 1
        for d in range(4):
            image = narrowed(parts[d]) * (STEP * factor)
            source = crop(d, q)
            if kind == 0:
                narrow[d, q] = image
                keep[d, q] = source + image
            elif kind == 1:
                narrow[d, q] = 4.0 * source + 17.0 / 9.0 * known[d, q] + image
            else:
                after = known[d, q] + source + image
                keep[d, q] = after
                narrow[d, q] = 0.25 * after - 17.0 / 36.0 * source

    vector_pass(WIDE_PAIRS, 2, rows_of(wide, first), row, *readers(base_w), vec_w, force_w, edge_w, total)
    link_pass(WIDE_PAIRS, force_w, write_wide)
    put_sums(sums, total, BLOCK, factor)
    factor_two = (8.0 / 9.0, 0.75, 1.0)[kind]

    def write_narrow(p, parts):
        for d in range(4):
            image = parts[d] * (STEP * factor_two)
            if kind == 0:
                after = keep[d, p] + image
                value = 0.25 * after - 17.0 / 36.0 * narrow[d, p]
                if after_out is not None:
                    put_block(after_out, d, p, after)
            elif kind == 1:
                value = image
            else:
                value = keep[d, p] + image
            put_block(out, d, p, value)

    vector_pass(NARROW_PAIRS, 1, rows_of(narrow), row_weights(weights, steps[1]), *readers(base_n),
                vec_n, force_n, edge_n, total)
    link_pass(NARROW_PAIRS, force_n, write_narrow)
    if other_sums is None:
        put_sums(sums, total, 2, factor_two, True)
    else:
        put_sums(other_sums, total, 2, factor_two)


def last_kernel(core, weights, *rest):
    blocks, rest = rest[:9], rest[9:]
    cos, cosines, sines, after, out, sums, wide, total, vec, force, edge, block, rows = rest
    assemble(core[0], blocks, wide)

    def sines_at(index, i):
        return roll(sines[index, i], -2, -2)

    def write(p, parts):
        for d in range(4):
            put_block(block, d, p, parts[d] * STEP)

    vector_pass(NARROW_PAIRS, 1, crop_of(wide), row_weights(weights, 0), crop_of(cos), crop_of(cosines), sines_at,
                vec, force, edge, total)
    link_pass(NARROW_PAIRS, force, write)
    put_sums(sums, total, 2, 1.0)

    def finish(first):
        for d in range(4):
            for t in range(2):
                at = (2 * d + t) * BLOCK
                rows[at:at + BLOCK] = block[d, first + t] + after[d, first + t]
        rows[...] = relabelled(rows[...], True)
        for d in range(4):
            for t in range(2):
                at = (2 * d + t) * BLOCK
                out[d, t] = rows[at:at + BLOCK]

    @pl.when(core[0] == 0)
    def _():
        finish(0)

    @pl.when(core[0] != 0)
    def _():
        finish(2)


VMEM = pl.BlockSpec(memory_space=pltpu.VMEM)
SMEM = pl.BlockSpec(memory_space=pltpu.SMEM)


def call(kernel, outs, scratch, scalars, arrays):
    return pl.pallas_call(
        kernel,
        out_shape=outs,
        in_specs=[SMEM] * len(scalars) + [VMEM] * len(arrays),
        out_specs=[VMEM] * len(outs),
        scratch_shapes=[pltpu.VMEM(shape.shape, F32) for shape in scratch],
        compiler_params=pltpu.CompilerParams(vmem_limit_bytes=18 * 2**20),
    )(*scalars, *arrays)


def base_shapes(wide):
    return [region(6, wide), region(12, wide, 1), OWN_SHAPE]


def forward(kind, steps, scalars, block, previous=None, keep=True):
    arrays = exchange(block) + ([] if previous is None else [previous])
    outs = [BLOCK_SHAPE, *base_shapes(True), *base_shapes(False)]
    scratch = [region(4, True), region(4, False)]
    for wide in (True, False):
        scratch += [region(6, wide), region(6, wide, 1), edge_region(wide)]
    if keep:
        outs = [region(4, False)] + outs
    else:
        scratch = [region(4, False)] + scratch

    def kernel(*refs):
        refs = list(refs)
        if not keep:
            at = 2 + len(arrays)
            refs.insert(at, refs.pop(at + len(outs)))
        forward_kernel(kind, steps, *refs)

    results = list(call(kernel, outs, scratch, scalars, arrays))
    narrow = results.pop(0) if keep else None
    out, *bases = results
    return narrow, out, bases[:3], bases[3:]


def backward(kind, steps, scalars, block, bases, known=None, wanted=()):
    fields = block.shape[0]
    arrays = exchange(block) + [array for base in bases for array in base]
    arrays += [] if known is None else [known]
    shapes = {"narrow": region(4, False), "out": BLOCK_SHAPE, "after": BLOCK_SHAPE, "sums": SUMS_SHAPE, "other": SUMS_SHAPE}
    names = [name for name in shapes if name in ("out", "sums") + tuple(wanted)]
    scratch = [region(fields, True), region(4, False), TOTAL_SHAPE]
    for wide in (True, False):
        scratch += [region(6, wide), region(6, wide, 1), edge_region(wide)]
    if fields == 8:
        scratch += [region(6, True), *base_shapes(True)]
    if "narrow" not in names:
        scratch.append(shapes["narrow"])

    def kernel(*refs):
        refs = list(refs)
        inputs, refs = refs[:2 + len(arrays)], refs[2 + len(arrays):]
        results = dict(zip(names, refs))
        refs = refs[len(names):]
        if "narrow" not in names:
            results["narrow"] = refs.pop()
        backward_kernel(kind, steps, *inputs, *[results.get(name) for name in shapes], *refs)

    return dict(zip(names, call(kernel, [shapes[name] for name in names], scratch, scalars, arrays)))


def last(scalars, block, base, after):
    scratch = [region(4, True), TOTAL_SHAPE, region(6, False), region(6, False, 1), edge_region(False),
               BLOCK_SHAPE, array_of(8 * BLOCK, 2 * HALF)]
    return call(last_kernel, [HOME_SHAPE, SUMS_SHAPE], scratch, scalars, [*exchange(block), *base, after])


def on_device(link_angles, cotangent, square_weight, oblong_weight):
    core = lax.axis_index("ta") % 2
    scalars = (core.reshape(1).astype(jnp.int32), jnp.concatenate([square_weight, oblong_weight], 1))
    own, = call(first_kernel, [array_of(8, 2, BLOCK, 2 * HALF)], [array_of(16 * BLOCK, 2 * HALF)], (), (link_angles, cotangent))
    own = permute(own, lambda t, x, c: (t, x, c), home, place)
    other = swap_cores(own)
    chip = jnp.concatenate([jnp.where(core == 0, own, other), jnp.where(core == 0, other, own)], 1)

    w1, b2, base_0, base_1 = forward(0, (0, 0), scalars, chip[:4])
    w3, b4, base_2, base_3 = forward(1, (0, 1), scalars, b2, w1)
    _, b6, base_4, base_5 = forward(2, (1, 1), scalars, b4, w3, False)
    _, b8, base_6, base_7 = forward(0, (2, 2), scalars, b6, None, False)

    two = backward(0, (2, 2), scalars, jnp.concatenate([b8, chip[4:]], 0), (base_7,), None, ("narrow",))
    mix = backward(1, (2, 1), scalars, two["out"], (base_6, base_5), two["narrow"], ("narrow", "other"))
    one = backward(2, (1, 1), scalars, mix["out"], (base_4, base_3), mix["narrow"])
    zero = backward(0, (0, 0), scalars, one["out"], (base_2, base_1), None, ("after",))
    result, sums = last(scalars, zero["out"], base_0, zero["after"])

    result = permute(result, lambda t, x, c: (t, x, c), place, home)

    steps = [sums + zero["sums"], one["sums"] + mix["other"], two["sums"] + mix["sums"]]
    rows = jnp.sum(jnp.stack(steps), (2, 3)).reshape(54) * (-0.5 * STEP)
    rows = jnp.broadcast_to(jnp.pad(rows, (0, HALF - 54))[None], (256, HALF))
    rows = lax.all_to_all(rows, ("ta", "gx"), 0, 0, tiled=True)
    sites = 16 * 8 * BLOCK * BLOCK * 2 * HALF
    totals = (jnp.sum(rows, 0)[:54] * (1.0 / math.sqrt(sites))).reshape(STEPS, 18)
    return result, totals[:, :6], totals[:, 6:]


def solution(mesh):
    in_specs = (P(None, "ta", "gx", None), P(None, "ta", "gx", None), P(), P())
    out_specs = (P(None, "ta", "gx", None), P(), P())
    return jax.shard_map(on_device, mesh=mesh, in_specs=in_specs, out_specs=out_specs, check_vma=False)
```

```python
import functools
import math

import jax
import jax.numpy as jnp
from jax import lax
from jax.experimental import pallas as pl
from jax.experimental.pallas import tpu as pltpu
from jax.sharding import PartitionSpec as P


Z = 16
STEPS = 3
STEP = 0.05
TURN = 2.0 * math.pi
PLANES = [(0, 1), (0, 2), (0, 3), (1, 2), (1, 3), (2, 3)]
BLOCK = 4
HALF = 128
F32 = jnp.float32

SIN = [4.442883014678955, -7.308241367340088, 3.6062889099121094, -0.8457635641098022, 0.10920574516057968]
COS = [1.4142135381698608, -6.978850841522217, 5.7394609451293945, -1.8835629224777222, 0.31069815158843994]


def oblong_index(first, second):
    return 6 + first * 3 + second - int(second > first)


def home(tau, xi, core):
    return ((tau % 16) * 2 + core) * 8 + xi % 8


def place(tau, xi, core):
    p = (tau + 12) % 16
    z, y_hi = (p, 0) if p < 8 else (15 - p, 1)
    xi = xi % 8
    x, side = (xi, 0) if xi < 4 else (7 - xi, 1)
    y_lo = side if y_hi == 0 else 1 - side
    return (z * 4 + y_hi * 2 + core) * 8 + y_lo * 4 + x


EVERY = [(t, x, c) for t in range(16) for x in range(8) for c in range(2)]


def permute(array, source, start=place, end=place):
    pairs = [(start(*source(t, x, c)), end(t, x, c)) for t, x, c in EVERY]
    return lax.ppermute(array, ("ta", "gx"), pairs)


def swap_cores(array):
    return permute(array, lambda t, x, c: (t, x, 1 - c))


SOURCES = [((-1, 0), (1, 0)), ((0, -1), (0, 1)), ((-1, -1), (1, 1)), ((1, -1), (-1, 1))]


def exchange(block):
    mine = []
    for choices in SOURCES:
        def source(t, x, c, choices=choices):
            return (t + choices[c][0], x + choices[c][1], 1 - c)
        mine.append(permute(block, source))
    mine = [mine[3], mine[2], jnp.concatenate(mine[:2], 1)]
    return [block, *mine, *[swap_cores(part) for part in mine]]


WIDE = 3


def roll(v, amount, axis):
    axis = axis % v.ndim
    return pltpu.roll(v, amount % v.shape[axis], axis)


def sublane(v):
    return lax.broadcasted_iota(jnp.int32, v.shape, v.ndim - 2)


def step_t(one, two):
    tiles = [one[1:2], two[0:1]]
    if one.shape[0] == WIDE:
        a, b = one[2:], two[2:]
        tiles.append(roll(jnp.where(sublane(a) < 4, b, a), 4, -2))
    return jnp.concatenate(tiles, 0)


def step_x(v, amount):
    if v.shape[0] != WIDE:
        return roll(v, -amount, -2)
    even, odd, rest = v[0:1], v[1:2], v[2:]
    at = sublane(rest)
    if amount > 0:
        moved = roll(rest, -1, -2)
        return jnp.concatenate([
            jnp.where(at == 7, moved, roll(even, -1, -2)),
            jnp.where(at == 7, roll(rest, 3, -2), roll(odd, -1, -2)),
            moved], 0)
    moved = roll(even, 1, -2)
    last = jnp.where(at == 4, roll(odd, -3, -2), roll(rest, 1, -2))
    return jnp.concatenate([moved, roll(odd, 1, -2), jnp.where(at == 0, moved, last)], 0)


def step_y(v, amount):
    yy = lax.broadcasted_iota(jnp.int32, v.shape, v.ndim - 1) % 8
    stays = yy < 7 if amount > 0 else yy > 0
    return jnp.where(stays, roll(v, -amount, -1), roll(v, 7 * amount, -1))


def shift(v, direction, amount):
    if direction == 1:
        return step_x(v, amount)
    if direction == 3:
        return roll(v, -8 * amount, -1)
    even, odd = v[:, 0], v[:, 1]
    if amount > 0:
        return jnp.stack([odd, step_y(even, 1)], 1)
    return jnp.stack([step_y(odd, -1), even], 1)


def narrowed(v):
    even, odd, rest = v[0:1], v[1:2], v[2:]
    inside = sublane(rest) < 6
    return jnp.concatenate([
        jnp.where(inside, roll(even, -2, -2), roll(rest, 6, -2)),
        jnp.where(inside, roll(odd, -2, -2), roll(rest, 2, -2))], 0)


def inner(v):
    return roll(v, -2, -2)[:, :, :BLOCK]


def sin_cos(turns):
    r = turns - jnp.round(turns)
    u = r * r
    s = SIN[-1]
    for a in SIN[-2::-1]:
        s = s * u + a
    c = COS[-1]
    for a in COS[-2::-1]:
        c = c * u + a
    s = s * r
    return s * c, 1.0 - s * s


def curls(here, ahead):
    for m, k in PLANES:
        moved = step_t(here[k], ahead[k]) if m == 0 else shift(here[k], m, 1)
        yield (here[m] - shift(here[m], k, 1)) + (moved - here[k])


def directions(j):
    m, k = PLANES[j]
    return [(m, oblong_index(m, k)), (k, oblong_index(k, m))]


def loop(first, last, body):
    def run(p, carry):
        body(p)
        return carry

    if last > first:
        lax.fori_loop(first, last, run, 0)


def schedule(pairs, own, first, second, third):
    def step(is_own, p, has_first, has_third):
        if has_third:
            third(p - 1)
        second(is_own, p)
        if has_first:
            first(p + 2)

    loop(0, 2, first)
    ranges = {}
    for p in range(pairs - 1):
        key = (own <= p < own + 2, p + 2 < pairs, third is not None and p >= 2)
        ranges.setdefault(key, []).append(p)
    for (is_own, has_first, has_third), at in ranges.items():
        loop(at[0], at[-1] + 1, lambda p, k=(is_own, has_first, has_third): step(k[0], p, k[1], k[2]))
    if third is not None:
        third(pairs - 2)


def add_back(total, value, j, direction, edge, weight):
    if direction == 0:
        back = step_t(edge[j], value)
        edge[j] = value
    else:
        back = shift(value, direction, -1)
    return total + weight * (value + back)


def base_pass(pairs, own, read, weights, sin, cos, cosines, sines, force=None, edge=None, write=None):
    def plaquettes(p):
        here = [read(d, p) for d in range(4)]
        ahead = [read(d, jnp.minimum(p + 1, pairs - 1)) for d in range(4)]
        for j, angle in enumerate(curls(here, ahead)):
            sin[j, p], cos[j, p] = sin_cos(angle)

    def forces(is_own, p):
        for j in range(6):
            s, c = sin[j, p], cos[j, p]
            if force is not None:
                total = weights[j] * s
            if is_own:
                sines[j, p - own] = s[:2]
            for direction, index in directions(j):
                if direction == 0:
                    s2, c2 = step_t(s, sin[j, p + 1]), step_t(c, cos[j, p + 1])
                else:
                    s2, c2 = shift(s, direction, 1), shift(c, direction, 1)
                cosines[index - 6, p] = c * c2 - s * s2
                if is_own or force is not None:
                    value = s * c2 + c * s2
                if is_own:
                    sines[index, p - own] = value[:2]
                if force is not None:
                    total = add_back(total, value, j, direction, edge, weights[index])
            if force is not None:
                force[j, p] = total

    schedule(pairs, own, plaquettes, forces, None if force is None else link_pass(force, write))


def vector_pass(pairs, own, read, weights, cos_at, cosines_at, sines_at, vec, force, edge, total, write):
    def plaquettes(p):
        here = [read(d, p) for d in range(4)]
        ahead = [read(d, jnp.minimum(p + 1, pairs - 1)) for d in range(4)]
        for j, value in enumerate(curls(here, ahead)):
            vec[j, p] = value

    total[...] = jnp.zeros(total.shape, F32)

    def forces(is_own, p):
        for j in range(6):
            q = vec[j, p]
            result = weights[j] * (cos_at(j, p) * q)
            if is_own:
                total[j] += jnp.sum(sines_at(j, p - own) * q[:2], 0)
            for direction, index in directions(j):
                both = q + (step_t(q, vec[j, p + 1]) if direction == 0 else shift(q, direction, 1))
                if is_own:
                    total[index] += jnp.sum(sines_at(index, p - own) * both[:2], 0)
                value = cosines_at(index - 6, p) * both
                result = add_back(result, value, j, direction, edge, weights[index])
            force[j, p] = result

    schedule(pairs, own, plaquettes, forces, link_pass(force, write))


def link_pass(force, write):
    def links(p):
        parts = [None] * 4
        for j, (m, k) in enumerate(PLANES):
            h = force[j, p]
            back_m = step_t(force[j, p - 1], h) if m == 0 else shift(h, m, -1)
            first, second = shift(h, k, -1) - h, h - back_m
            parts[m] = first if parts[m] is None else parts[m] + first
            parts[k] = second if parts[k] is None else parts[k] + second
        write(p, parts)

    return links


WIDE_PAIRS = 6
NARROW_PAIRS = 4


def region(fields, wide, cut=0):
    pairs, tiles = (WIDE_PAIRS, WIDE) if wide else (NARROW_PAIRS, 2)
    return jax.ShapeDtypeStruct((fields, pairs - cut, tiles, 2, 8, HALF), F32)


def edge_region(wide):
    return jax.ShapeDtypeStruct((3, WIDE if wide else 2, 2, 8, HALF), F32)


def array_of(*shape):
    return jax.ShapeDtypeStruct(shape, F32)


HOME_SHAPE = array_of(4, 2, BLOCK, 2 * HALF)
BLOCK_SHAPE = array_of(4, BLOCK, BLOCK, 2 * HALF)
OWN_SHAPE = array_of(18, 2, 2, 2, 8, HALF)
SUMS_SHAPE = array_of(18, 8, HALF)
TOTAL_SHAPE = array_of(18, 2, 8, HALF)


def relabelled(rows, back):
    old = lax.broadcasted_iota(jnp.int32, (2 * HALF, 2 * HALF), 1 if back else 0)
    new = lax.broadcasted_iota(jnp.int32, (2 * HALF, 2 * HALF), 0 if back else 1)
    y, z = 2 * (new % 8) + new // HALF, (new % HALF) // 8
    matrix = jnp.where(old == y * Z + z, 1.0, 0.0).astype(F32)
    return lax.dot(rows, matrix, precision=lax.Precision.HIGHEST, preferred_element_type=F32)


def first_kernel(links, cotangent, out, rows):
    for f in range(8):
        for t in range(2):
            value = links[f, t] * (1.0 / TURN) if f < 4 else cotangent[f - 4, t]
            rows[(2 * f + t) * BLOCK:(2 * f + t + 1) * BLOCK] = value
    rows[...] = relabelled(rows[...], False)
    for f in range(8):
        for t in range(2):
            out[f, t] = rows[(2 * f + t) * BLOCK:(2 * f + t + 1) * BLOCK]


def assemble(core, blocks, wide):
    def put(row, column, block, first=0):
        for i in range(BLOCK):
            odd = i % 2
            tile = odd if column < 2 else 2
            x = BLOCK * (column if column < 2 else odd)
            for h in range(2):
                part = block[:, first + i, :, h * HALF:(h + 1) * HALF]
                wide[:, 2 * row + i // 2, tile, h, x:x + BLOCK, :] = part

    def fill(left, right):
        where = ((2, 0), (2, BLOCK), (1, 0), (0, 0))
        for (i, first), row, column in zip(where, (0, 1, 0, 2), (1, 0, 0, 0)):
            put(row, column, left[i], first)
        for (i, first), row, column in zip(where, (2, 1, 2, 0), (1, 2, 2, 2)):
            put(row, column, right[i], first)

    put(1, 1, blocks[0])

    @pl.when(core == 0)
    def _():
        fill(blocks[1:4], blocks[4:])

    @pl.when(core != 0)
    def _():
        fill(blocks[4:], blocks[1:4])


def rows_of(ref, first=0):
    return lambda d, p: ref[first + d, p]


def crop_of(ref, first=0):
    return lambda d, p: narrowed(ref[first + d, p + 1])


def put_block(out, d, p, v):
    at = pl.ds(2 * p - 2, 2)
    v = inner(v)
    out[d, at, :, :HALF] = v[:, 0]
    out[d, at, :, HALF:] = v[:, 1]


def row_weights(weights, step):
    return [weights[step, j] for j in range(18)]


def forward_kernel(kind, steps, core, weights, *rest):
    blocks, rest = rest[:7], list(rest[7:])
    previous = rest.pop(0) if kind else None
    narrow, out, cos_w, cosines_w, sines_w, cos_n, cosines_n, sines_n = rest[:8]
    wide, drift, sin_w, force_w, edge_w, sin_n, force_n, edge_n = rest[8:]
    assemble(core[0], blocks, wide)
    crop = crop_of(wide)
    unit = STEP / TURN

    def write_wide(p, parts):
        q = p - 1
        for d in range(4):
            z = narrowed(parts[d]) * unit
            if kind == 0:
                drift[d, q] = z
                narrow[d, q] = crop(d, q) + 0.25 * z
            elif kind == 1:
                narrow[d, q] = previous[d, q] + 0.75 * z
            else:
                second = crop(d, q)
                narrow[d, q] = second + 8.0 / 9.0 * z - 17.0 / 9.0 * (second - previous[d, q])

    base_pass(WIDE_PAIRS, 2, rows_of(wide), row_weights(weights, steps[0]),
              sin_w, cos_w, cosines_w, sines_w, force_w, edge_w, write_wide)

    def write_narrow(p, parts):
        for d in range(4):
            z = parts[d] * unit
            if kind == 0:
                value = narrow[d, p] + 8.0 / 9.0 * z - 17.0 / 36.0 * drift[d, p]
            elif kind == 1:
                value = narrow[d, p] + 0.25 * z
            else:
                value = crop(d, p) + 0.75 * z
            put_block(out, d, p, value)

    base_pass(NARROW_PAIRS, 1, rows_of(narrow), row_weights(weights, steps[1]),
              sin_n, cos_n, cosines_n, sines_n, force_n, edge_n, write_narrow)


def put_sums(out, total, first, factor, add=False):
    x = lax.broadcasted_iota(jnp.int32, (8, HALF), 0)
    kept = (x >= first) & (x < first + BLOCK)
    for index in range(18):
        value = jnp.where(kept, (total[index, 0] + total[index, 1]) * factor, 0.0)
        out[index] = out[index] + value if add else value


def readers(base):
    return [rows_of(ref) for ref in base]


def backward_kernel(kind, steps, core, weights, *rest):
    blocks, rest = rest[:7], list(rest[7:])
    first = blocks[0].shape[0] - 4
    base_w = None if first else [rest.pop(0) for _ in range(3)]
    base_n = [rest.pop(0) for _ in range(3)]
    known = rest.pop(0) if kind else None
    narrow, out, after_out, sums, other_sums = [rest.pop(0) for _ in range(5)]
    wide, keep, total, vec_w, force_w, edge_w, vec_n, force_n, edge_n, *base_scratch = rest
    assemble(core[0], blocks, wide)
    row = row_weights(weights, steps[0])
    if first:
        sin_w, *base_w = base_scratch
        base_pass(WIDE_PAIRS, 2, rows_of(wide), row, sin_w, *base_w)
    crop = crop_of(wide, first)
    factor = (0.75, 1.0, 8.0 / 9.0)[kind]

    def write_wide(p, parts):
        q = p - 1
        for d in range(4):
            image = narrowed(parts[d]) * (STEP * factor)
            source = crop(d, q)
            if kind == 0:
                narrow[d, q] = image
                keep[d, q] = source + image
            elif kind == 1:
                narrow[d, q] = 4.0 * source + 17.0 / 9.0 * known[d, q] + image
            else:
                after = known[d, q] + source + image
                keep[d, q] = after
                narrow[d, q] = 0.25 * after - 17.0 / 36.0 * source

    vector_pass(WIDE_PAIRS, 2, rows_of(wide, first), row, *readers(base_w),
                vec_w, force_w, edge_w, total, write_wide)
    put_sums(sums, total, BLOCK, factor)
    factor_two = (8.0 / 9.0, 0.75, 1.0)[kind]

    def write_narrow(p, parts):
        for d in range(4):
            image = parts[d] * (STEP * factor_two)
            if kind == 0:
                after = keep[d, p] + image
                value = 0.25 * after - 17.0 / 36.0 * narrow[d, p]
                if after_out is not None:
                    put_block(after_out, d, p, after)
            elif kind == 1:
                value = image
            else:
                value = keep[d, p] + image
            put_block(out, d, p, value)

    vector_pass(NARROW_PAIRS, 1, rows_of(narrow), row_weights(weights, steps[1]), *readers(base_n),
                vec_n, force_n, edge_n, total, write_narrow)
    if other_sums is None:
        put_sums(sums, total, 2, factor_two, True)
    else:
        put_sums(other_sums, total, 2, factor_two)


def last_kernel(core, weights, *rest):
    blocks, rest = rest[:7], rest[7:]
    cos, cosines, sines, after, out, sums, wide, total, vec, force, edge, block, rows = rest
    assemble(core[0], blocks, wide)

    def sines_at(index, i):
        return roll(sines[index, i], -2, -2)

    def write(p, parts):
        for d in range(4):
            put_block(block, d, p, parts[d] * STEP)

    vector_pass(NARROW_PAIRS, 1, crop_of(wide), row_weights(weights, 0), crop_of(cos), crop_of(cosines), sines_at,
                vec, force, edge, total, write)
    put_sums(sums, total, 2, 1.0)

    def finish(first):
        for d in range(4):
            for t in range(2):
                at = (2 * d + t) * BLOCK
                rows[at:at + BLOCK] = block[d, first + t] + after[d, first + t]
        rows[...] = relabelled(rows[...], True)
        for d in range(4):
            for t in range(2):
                at = (2 * d + t) * BLOCK
                out[d, t] = rows[at:at + BLOCK]

    @pl.when(core[0] == 0)
    def _():
        finish(0)

    @pl.when(core[0] != 0)
    def _():
        finish(2)


VMEM = pl.BlockSpec(memory_space=pltpu.VMEM)
SMEM = pl.BlockSpec(memory_space=pltpu.SMEM)


def call(kernel, outs, scratch, scalars, arrays):
    return pl.pallas_call(
        kernel,
        out_shape=outs,
        in_specs=[SMEM] * len(scalars) + [VMEM] * len(arrays),
        out_specs=[VMEM] * len(outs),
        scratch_shapes=[pltpu.VMEM(shape.shape, F32) for shape in scratch],
        compiler_params=pltpu.CompilerParams(vmem_limit_bytes=18 * 2**20),
    )(*scalars, *arrays)


def base_shapes(wide):
    return [region(6, wide), region(12, wide, 1), OWN_SHAPE]


def forward(kind, steps, scalars, block, previous=None, keep=True):
    arrays = exchange(block) + ([] if previous is None else [previous])
    outs = [BLOCK_SHAPE, *base_shapes(True), *base_shapes(False)]
    scratch = [region(4, True), region(4, False)]
    for wide in (True, False):
        scratch += [region(6, wide), region(6, wide, 1), edge_region(wide)]
    if keep:
        outs = [region(4, False)] + outs
    else:
        scratch = [region(4, False)] + scratch

    def kernel(*refs):
        refs = list(refs)
        if not keep:
            at = 2 + len(arrays)
            refs.insert(at, refs.pop(at + len(outs)))
        forward_kernel(kind, steps, *refs)

    results = list(call(kernel, outs, scratch, scalars, arrays))
    narrow = results.pop(0) if keep else None
    out, *bases = results
    return narrow, out, bases[:3], bases[3:]


def backward(kind, steps, scalars, block, bases, known=None, wanted=()):
    fields = block.shape[0]
    arrays = exchange(block) + [array for base in bases for array in base]
    arrays += [] if known is None else [known]
    shapes = {"narrow": region(4, False), "out": BLOCK_SHAPE, "after": BLOCK_SHAPE, "sums": SUMS_SHAPE, "other": SUMS_SHAPE}
    names = [name for name in shapes if name in ("out", "sums") + tuple(wanted)]
    scratch = [region(fields, True), region(4, False), TOTAL_SHAPE]
    for wide in (True, False):
        scratch += [region(6, wide), region(6, wide, 1), edge_region(wide)]
    if fields == 8:
        scratch += [region(6, True), *base_shapes(True)]
    if "narrow" not in names:
        scratch.append(shapes["narrow"])

    def kernel(*refs):
        refs = list(refs)
        inputs, refs = refs[:2 + len(arrays)], refs[2 + len(arrays):]
        results = dict(zip(names, refs))
        refs = refs[len(names):]
        if "narrow" not in names:
            results["narrow"] = refs.pop()
        backward_kernel(kind, steps, *inputs, *[results.get(name) for name in shapes], *refs)

    return dict(zip(names, call(kernel, [shapes[name] for name in names], scratch, scalars, arrays)))


def last(scalars, block, base, after):
    scratch = [region(4, True), TOTAL_SHAPE, region(6, False), region(6, False, 1), edge_region(False),
               BLOCK_SHAPE, array_of(8 * BLOCK, 2 * HALF)]
    return call(last_kernel, [HOME_SHAPE, SUMS_SHAPE], scratch, scalars, [*exchange(block), *base, after])


def on_device(link_angles, cotangent, square_weight, oblong_weight):
    core = lax.axis_index("ta") % 2
    scalars = (core.reshape(1).astype(jnp.int32), jnp.concatenate([square_weight, oblong_weight], 1))
    own, = call(first_kernel, [array_of(8, 2, BLOCK, 2 * HALF)], [array_of(16 * BLOCK, 2 * HALF)], (), (link_angles, cotangent))
    own = permute(own, lambda t, x, c: (t, x, c), home, place)
    other = swap_cores(own)
    chip = jnp.concatenate([jnp.where(core == 0, own, other), jnp.where(core == 0, other, own)], 1)

    w1, b2, base_0, base_1 = forward(0, (0, 0), scalars, chip[:4])
    w3, b4, base_2, base_3 = forward(1, (0, 1), scalars, b2, w1)
    _, b6, base_4, base_5 = forward(2, (1, 1), scalars, b4, w3, False)
    _, b8, base_6, base_7 = forward(0, (2, 2), scalars, b6, None, False)

    two = backward(0, (2, 2), scalars, jnp.concatenate([b8, chip[4:]], 0), (base_7,), None, ("narrow",))
    mix = backward(1, (2, 1), scalars, two["out"], (base_6, base_5), two["narrow"], ("narrow", "other"))
    one = backward(2, (1, 1), scalars, mix["out"], (base_4, base_3), mix["narrow"])
    zero = backward(0, (0, 0), scalars, one["out"], (base_2, base_1), None, ("after",))
    result, sums = last(scalars, zero["out"], base_0, zero["after"])

    result = permute(result, lambda t, x, c: (t, x, c), place, home)

    steps = [sums + zero["sums"], one["sums"] + mix["other"], two["sums"] + mix["sums"]]
    rows = jnp.sum(jnp.stack(steps), (2, 3)).reshape(54) * (-0.5 * STEP)
    rows = jnp.broadcast_to(jnp.pad(rows, (0, HALF - 54))[None], (256, HALF))
    rows = lax.all_to_all(rows, ("ta", "gx"), 0, 0, tiled=True)
    sites = 16 * 8 * BLOCK * BLOCK * 2 * HALF
    totals = (jnp.sum(rows, 0)[:54] * (1.0 / math.sqrt(sites))).reshape(STEPS, 18)
    return result, totals[:, :6], totals[:, 6:]


def solution(mesh):
    in_specs = (P(None, "ta", "gx", None), P(None, "ta", "gx", None), P(), P())
    out_specs = (P(None, "ta", "gx", None), P(), P())
    return jax.shard_map(on_device, mesh=mesh, in_specs=in_specs, out_specs=out_specs, check_vma=False)
```

```python
import functools
import itertools
import math

import jax
import jax.numpy as jnp
from jax import lax
from jax.experimental import pallas as pl
from jax.experimental.pallas import tpu as pltpu
from jax.sharding import PartitionSpec as P


Z = 16
STEPS = 3
STEP = 0.05
TURN = 2.0 * math.pi
PLANES = [(0, 1), (0, 2), (0, 3), (1, 2), (1, 3), (2, 3)]
BLOCK = 4
HALF = 128
F32 = jnp.float32

SIN = [4.442883014678955, -7.308241367340088, 3.6062889099121094, -0.8457635641098022, 0.10920574516057968]
COS = [1.4142135381698608, -6.978850841522217, 5.7394609451293945, -1.8835629224777222, 0.31069815158843994]


def oblong_index(first, second):
    return 6 + first * 3 + second - int(second > first)


def home(tau, xi, core):
    return ((tau % 16) * 2 + core) * 8 + xi % 8


def place(tau, xi, core):
    p = (tau + 12) % 16
    z, y_hi = (p, 0) if p < 8 else (15 - p, 1)
    xi = xi % 8
    x, side = (xi, 0) if xi < 4 else (7 - xi, 1)
    y_lo = side if y_hi == 0 else 1 - side
    return (z * 4 + y_hi * 2 + core) * 8 + y_lo * 4 + x


EVERY = [(t, x, c) for t in range(16) for x in range(8) for c in range(2)]


def permute(array, source, start=place, end=place):
    pairs = [(start(*source(t, x, c)), end(t, x, c)) for t, x, c in EVERY]
    return lax.ppermute(array, ("ta", "gx"), pairs)


def swap_cores(array):
    return permute(array, lambda t, x, c: (t, x, 1 - c))


SOURCES = [((-1, 0), (1, 0)), ((0, -1), (0, 1)), ((-1, -1), (1, 1)), ((1, -1), (-1, 1))]


def exchange(block):
    mine = []
    for choices in SOURCES:
        def source(t, x, c, choices=choices):
            return (t + choices[c][0], x + choices[c][1], 1 - c)
        mine.append(permute(block, source))
    mine = [mine[3], mine[2], jnp.concatenate(mine[:2], 1)]
    return [block, *mine, *[swap_cores(part) for part in mine]]


WIDE = 3


def roll(v, amount, axis):
    axis = axis % v.ndim
    return pltpu.roll(v, amount % v.shape[axis], axis)


def sublane(v):
    return lax.broadcasted_iota(jnp.int32, v.shape, v.ndim - 2)


def step_t(one, two):
    tiles = [one[1:2], two[0:1]]
    if one.shape[0] == WIDE:
        a, b = one[2:], two[2:]
        tiles.append(roll(jnp.where(sublane(a) < 4, b, a), 4, -2))
    return jnp.concatenate(tiles, 0)


def step_x(v, amount):
    if v.shape[0] != WIDE:
        return roll(v, -amount, -2)
    even, odd, rest = v[0:1], v[1:2], v[2:]
    at = sublane(rest)
    if amount > 0:
        moved = roll(rest, -1, -2)
        return jnp.concatenate([
            jnp.where(at == 7, moved, roll(even, -1, -2)),
            jnp.where(at == 7, roll(rest, 3, -2), roll(odd, -1, -2)),
            moved], 0)
    moved = roll(even, 1, -2)
    last = jnp.where(at == 4, roll(odd, -3, -2), roll(rest, 1, -2))
    return jnp.concatenate([moved, roll(odd, 1, -2), jnp.where(at == 0, moved, last)], 0)


def step_y(v, amount):
    yy = lax.broadcasted_iota(jnp.int32, v.shape, v.ndim - 1) % 8
    stays = yy < 7 if amount > 0 else yy > 0
    return jnp.where(stays, roll(v, -amount, -1), roll(v, 7 * amount, -1))


def shift(v, direction, amount):
    if direction == 1:
        return step_x(v, amount)
    if direction == 3:
        return roll(v, -8 * amount, -1)
    even, odd = v[:, 0], v[:, 1]
    if amount > 0:
        return jnp.stack([odd, step_y(even, 1)], 1)
    return jnp.stack([step_y(odd, -1), even], 1)


def narrowed(v):
    even, odd, rest = v[0:1], v[1:2], v[2:]
    inside = sublane(rest) < 6
    return jnp.concatenate([
        jnp.where(inside, roll(even, -2, -2), roll(rest, 6, -2)),
        jnp.where(inside, roll(odd, -2, -2), roll(rest, 2, -2))], 0)


def inner(v):
    return roll(v, -2, -2)[:, :, :BLOCK]


def sin_cos(turns):
    r = turns - jnp.round(turns)
    u = r * r
    s = SIN[-1]
    for a in SIN[-2::-1]:
        s = s * u + a
    c = COS[-1]
    for a in COS[-2::-1]:
        c = c * u + a
    s = s * r
    return s * c, 1.0 - s * s


def curls(here, ahead):
    for m, k in PLANES:
        moved = step_t(here[k], ahead[k]) if m == 0 else shift(here[k], m, 1)
        yield (here[m] - shift(here[m], k, 1)) + (moved - here[k])


def directions(j):
    m, k = PLANES[j]
    return [(m, oblong_index(m, k)), (k, oblong_index(k, m))]


def loop(first, last, body):
    def turn(p, carry):
        body(p)
        return carry

    if last > first:
        lax.fori_loop(first, last, turn, 0)


def run(*passes, together=True):
    for _ in itertools.zip_longest(*passes) if together else itertools.chain(*passes):
        pass


def schedule(pairs, own, first, second, third):
    def step(is_own, p, has_first, has_third):
        passes = [third(p - 1)] if has_third else []
        passes.append(second(is_own, p))
        if has_first:
            passes.append(first(p + 2))
        run(*passes, together=has_first and pairs == WIDE_PAIRS)

    loop(0, 2, lambda p: run(first(p)))
    ranges = {}
    for p in range(pairs - 1):
        key = (own <= p < own + 2, p + 2 < pairs, third is not None and p >= 2)
        ranges.setdefault(key, []).append(p)
    for (is_own, has_first, has_third), at in ranges.items():
        loop(at[0], at[-1] + 1, lambda p, k=(is_own, has_first, has_third): step(k[0], p, k[1], k[2]))
    if third is not None:
        run(third(pairs - 2))


def add_back(total, value, j, direction, edge, weight):
    if direction == 0:
        back = step_t(edge[j], value)
        edge[j] = value
    else:
        back = shift(value, direction, -1)
    return total + weight * (value + back)


def base_pass(pairs, own, read, weights, sin, cos, cosines, sines, force=None, edge=None, write=None):
    def plaquettes(p):
        here = [read(d, p) for d in range(4)]
        ahead = [read(d, jnp.minimum(p + 1, pairs - 1)) for d in range(4)]
        for j, angle in enumerate(curls(here, ahead)):
            sin[j, p], cos[j, p] = sin_cos(angle)
            yield

    def forces(is_own, p):
        for j in range(6):
            s, c = sin[j, p], cos[j, p]
            if force is not None:
                total = weights[j] * s
            if is_own:
                sines[j, p - own] = s[:2]
            for direction, index in directions(j):
                if direction == 0:
                    s2, c2 = step_t(s, sin[j, p + 1]), step_t(c, cos[j, p + 1])
                else:
                    s2, c2 = shift(s, direction, 1), shift(c, direction, 1)
                cosines[index - 6, p] = c * c2 - s * s2
                if is_own or force is not None:
                    value = s * c2 + c * s2
                if is_own:
                    sines[index, p - own] = value[:2]
                if force is not None:
                    total = add_back(total, value, j, direction, edge, weights[index])
            if force is not None:
                force[j, p] = total
            yield

    schedule(pairs, own, plaquettes, forces, None if force is None else link_pass(force, write))


def vector_pass(pairs, own, read, weights, cos_at, cosines_at, sines_at, vec, force, edge, total, write):
    def plaquettes(p):
        here = [read(d, p) for d in range(4)]
        ahead = [read(d, jnp.minimum(p + 1, pairs - 1)) for d in range(4)]
        for j, value in enumerate(curls(here, ahead)):
            vec[j, p] = value
            yield

    total[...] = jnp.zeros(total.shape, F32)

    def forces(is_own, p):
        for j in range(6):
            q = vec[j, p]
            result = weights[j] * (cos_at(j, p) * q)
            if is_own:
                total[j] += jnp.sum(sines_at(j, p - own) * q[:2], 0)
            for direction, index in directions(j):
                both = q + (step_t(q, vec[j, p + 1]) if direction == 0 else shift(q, direction, 1))
                if is_own:
                    total[index] += jnp.sum(sines_at(index, p - own) * both[:2], 0)
                value = cosines_at(index - 6, p) * both
                result = add_back(result, value, j, direction, edge, weights[index])
            force[j, p] = result
            yield

    schedule(pairs, own, plaquettes, forces, link_pass(force, write))


def link_pass(force, write):
    def links(p):
        parts = [None] * 4
        for j, (m, k) in enumerate(PLANES):
            h = force[j, p]
            back_m = step_t(force[j, p - 1], h) if m == 0 else shift(h, m, -1)
            first, second = shift(h, k, -1) - h, h - back_m
            parts[m] = first if parts[m] is None else parts[m] + first
            parts[k] = second if parts[k] is None else parts[k] + second
            yield
        write(p, parts)

    return links


WIDE_PAIRS = 6
NARROW_PAIRS = 4


def region(fields, wide, cut=0):
    pairs, tiles = (WIDE_PAIRS, WIDE) if wide else (NARROW_PAIRS, 2)
    return jax.ShapeDtypeStruct((fields, pairs - cut, tiles, 2, 8, HALF), F32)


def edge_region(wide):
    return jax.ShapeDtypeStruct((3, WIDE if wide else 2, 2, 8, HALF), F32)


def array_of(*shape):
    return jax.ShapeDtypeStruct(shape, F32)


HOME_SHAPE = array_of(4, 2, BLOCK, 2 * HALF)
BLOCK_SHAPE = array_of(4, BLOCK, BLOCK, 2 * HALF)
OWN_SHAPE = array_of(18, 2, 2, 2, 8, HALF)
SUMS_SHAPE = array_of(18, 8, HALF)
TOTAL_SHAPE = array_of(18, 2, 8, HALF)


def relabelled(rows, back):
    old = lax.broadcasted_iota(jnp.int32, (2 * HALF, 2 * HALF), 1 if back else 0)
    new = lax.broadcasted_iota(jnp.int32, (2 * HALF, 2 * HALF), 0 if back else 1)
    y, z = 2 * (new % 8) + new // HALF, (new % HALF) // 8
    matrix = jnp.where(old == y * Z + z, 1.0, 0.0).astype(F32)
    return lax.dot(rows, matrix, precision=lax.Precision.HIGHEST, preferred_element_type=F32)


def first_kernel(links, cotangent, out, rows):
    for f in range(8):
        for t in range(2):
            value = links[f, t] * (1.0 / TURN) if f < 4 else cotangent[f - 4, t]
            rows[(2 * f + t) * BLOCK:(2 * f + t + 1) * BLOCK] = value
    rows[...] = relabelled(rows[...], False)
    for f in range(8):
        for t in range(2):
            out[f, t] = rows[(2 * f + t) * BLOCK:(2 * f + t + 1) * BLOCK]


def assemble(core, blocks, wide):
    def put(row, column, block, first=0):
        for i in range(BLOCK):
            odd = i % 2
            tile = odd if column < 2 else 2
            x = BLOCK * (column if column < 2 else odd)
            for h in range(2):
                part = block[:, first + i, :, h * HALF:(h + 1) * HALF]
                wide[:, 2 * row + i // 2, tile, h, x:x + BLOCK, :] = part

    def fill(left, right):
        where = ((2, 0), (2, BLOCK), (1, 0), (0, 0))
        for (i, first), row, column in zip(where, (0, 1, 0, 2), (1, 0, 0, 0)):
            put(row, column, left[i], first)
        for (i, first), row, column in zip(where, (2, 1, 2, 0), (1, 2, 2, 2)):
            put(row, column, right[i], first)

    put(1, 1, blocks[0])

    @pl.when(core == 0)
    def _():
        fill(blocks[1:4], blocks[4:])

    @pl.when(core != 0)
    def _():
        fill(blocks[4:], blocks[1:4])


def rows_of(ref, first=0):
    return lambda d, p: ref[first + d, p]


def crop_of(ref, first=0):
    return lambda d, p: narrowed(ref[first + d, p + 1])


def put_block(out, d, p, v):
    at = pl.ds(2 * p - 2, 2)
    v = inner(v)
    out[d, at, :, :HALF] = v[:, 0]
    out[d, at, :, HALF:] = v[:, 1]


def row_weights(weights, step):
    return [weights[step, j] for j in range(18)]


def forward_kernel(kind, steps, core, weights, *rest):
    blocks, rest = rest[:7], list(rest[7:])
    previous = rest.pop(0) if kind else None
    narrow, out, cos_w, cosines_w, sines_w, cos_n, cosines_n, sines_n = rest[:8]
    wide, drift, sin_w, force_w, edge_w, sin_n, force_n, edge_n = rest[8:]
    assemble(core[0], blocks, wide)
    crop = crop_of(wide)
    unit = STEP / TURN

    def write_wide(p, parts):
        q = p - 1
        for d in range(4):
            z = narrowed(parts[d]) * unit
            if kind == 0:
                drift[d, q] = z
                narrow[d, q] = crop(d, q) + 0.25 * z
            elif kind == 1:
                narrow[d, q] = previous[d, q] + 0.75 * z
            else:
                second = crop(d, q)
                narrow[d, q] = second + 8.0 / 9.0 * z - 17.0 / 9.0 * (second - previous[d, q])

    base_pass(WIDE_PAIRS, 2, rows_of(wide), row_weights(weights, steps[0]),
              sin_w, cos_w, cosines_w, sines_w, force_w, edge_w, write_wide)

    def write_narrow(p, parts):
        for d in range(4):
            z = parts[d] * unit
            if kind == 0:
                value = narrow[d, p] + 8.0 / 9.0 * z - 17.0 / 36.0 * drift[d, p]
            elif kind == 1:
                value = narrow[d, p] + 0.25 * z
            else:
                value = crop(d, p) + 0.75 * z
            put_block(out, d, p, value)

    base_pass(NARROW_PAIRS, 1, rows_of(narrow), row_weights(weights, steps[1]),
              sin_n, cos_n, cosines_n, sines_n, force_n, edge_n, write_narrow)


def put_sums(out, total, first, factor, add=False):
    x = lax.broadcasted_iota(jnp.int32, (8, HALF), 0)
    kept = (x >= first) & (x < first + BLOCK)
    for index in range(18):
        value = jnp.where(kept, (total[index, 0] + total[index, 1]) * factor, 0.0)
        out[index] = out[index] + value if add else value


def readers(base):
    return [rows_of(ref) for ref in base]


def backward_kernel(kind, steps, core, weights, *rest):
    blocks, rest = rest[:7], list(rest[7:])
    first = blocks[0].shape[0] - 4
    base_w = None if first else [rest.pop(0) for _ in range(3)]
    base_n = [rest.pop(0) for _ in range(3)]
    known = rest.pop(0) if kind else None
    narrow, out, after_out, sums, other_sums = [rest.pop(0) for _ in range(5)]
    wide, keep, total, vec_w, force_w, edge_w, vec_n, force_n, edge_n, *base_scratch = rest
    assemble(core[0], blocks, wide)
    row = row_weights(weights, steps[0])
    if first:
        sin_w, *base_w = base_scratch
        base_pass(WIDE_PAIRS, 2, rows_of(wide), row, sin_w, *base_w)
    crop = crop_of(wide, first)
    factor = (0.75, 1.0, 8.0 / 9.0)[kind]

    def write_wide(p, parts):
        q = p - 1
        for d in range(4):
            image = narrowed(parts[d]) * (STEP * factor)
            source = crop(d, q)
            if kind == 0:
                narrow[d, q] = image
                keep[d, q] = source + image
            elif kind == 1:
                narrow[d, q] = 4.0 * source + 17.0 / 9.0 * known[d, q] + image
            else:
                after = known[d, q] + source + image
                keep[d, q] = after
                narrow[d, q] = 0.25 * after - 17.0 / 36.0 * source

    vector_pass(WIDE_PAIRS, 2, rows_of(wide, first), row, *readers(base_w),
                vec_w, force_w, edge_w, total, write_wide)
    put_sums(sums, total, BLOCK, factor)
    factor_two = (8.0 / 9.0, 0.75, 1.0)[kind]

    def write_narrow(p, parts):
        for d in range(4):
            image = parts[d] * (STEP * factor_two)
            if kind == 0:
                after = keep[d, p] + image
                value = 0.25 * after - 17.0 / 36.0 * narrow[d, p]
                if after_out is not None:
                    put_block(after_out, d, p, after)
            elif kind == 1:
                value = image
            else:
                value = keep[d, p] + image
            put_block(out, d, p, value)

    vector_pass(NARROW_PAIRS, 1, rows_of(narrow), row_weights(weights, steps[1]), *readers(base_n),
                vec_n, force_n, edge_n, total, write_narrow)
    if other_sums is None:
        put_sums(sums, total, 2, factor_two, True)
    else:
        put_sums(other_sums, total, 2, factor_two)


def last_kernel(core, weights, *rest):
    blocks, rest = rest[:7], rest[7:]
    cos, cosines, sines, after, zero, one, mix_one, mix_two, two = rest[:9]
    out, sent, wide, total, vec, force, edge, block, rows, sums, terms = rest[9:]
    assemble(core[0], blocks, wide)

    def sines_at(index, i):
        return roll(sines[index, i], -2, -2)

    def write(p, parts):
        for d in range(4):
            put_block(block, d, p, parts[d] * STEP)

    vector_pass(NARROW_PAIRS, 1, crop_of(wide), row_weights(weights, 0), crop_of(cos), crop_of(cosines), sines_at,
                vec, force, edge, total, write)
    put_sums(sums, total, 2, 1.0)
    terms[...] = jnp.zeros(terms.shape, F32)
    for step, parts in enumerate(((sums, zero), (one, mix_one), (two, mix_two))):
        both = parts[0][...] + parts[1][...]
        terms[18 * step:18 * step + 18, :] = jnp.sum(both, 1) * (-0.5 * STEP)
    row = lax.dot_general(jnp.ones((8, HALF), F32), terms[...], (((1,), (1,)), ((), ())),
                          precision=lax.Precision.HIGHEST, preferred_element_type=F32)
    sent[...] = jnp.broadcast_to(row[None, :1], sent.shape)

    def finish(first):
        for d in range(4):
            for t in range(2):
                at = (2 * d + t) * BLOCK
                rows[at:at + BLOCK] = block[d, first + t] + after[d, first + t]
        rows[...] = relabelled(rows[...], True)
        for d in range(4):
            for t in range(2):
                at = (2 * d + t) * BLOCK
                out[d, t] = rows[at:at + BLOCK]

    @pl.when(core[0] == 0)
    def _():
        finish(0)

    @pl.when(core[0] != 0)
    def _():
        finish(2)


VMEM = pl.BlockSpec(memory_space=pltpu.VMEM)
SMEM = pl.BlockSpec(memory_space=pltpu.SMEM)


def call(kernel, outs, scratch, scalars, arrays):
    return pl.pallas_call(
        kernel,
        out_shape=outs,
        in_specs=[SMEM] * len(scalars) + [VMEM] * len(arrays),
        out_specs=[VMEM] * len(outs),
        scratch_shapes=[pltpu.VMEM(shape.shape, F32) for shape in scratch],
        compiler_params=pltpu.CompilerParams(vmem_limit_bytes=18 * 2**20),
    )(*scalars, *arrays)


def base_shapes(wide):
    return [region(6, wide), region(12, wide, 1), OWN_SHAPE]


def forward(kind, steps, scalars, block, previous=None, keep=True):
    arrays = exchange(block) + ([] if previous is None else [previous])
    outs = [BLOCK_SHAPE, *base_shapes(True), *base_shapes(False)]
    scratch = [region(4, True), region(4, False)]
    for wide in (True, False):
        scratch += [region(6, wide), region(6, wide, 1), edge_region(wide)]
    if keep:
        outs = [region(4, False)] + outs
    else:
        scratch = [region(4, False)] + scratch

    def kernel(*refs):
        refs = list(refs)
        if not keep:
            at = 2 + len(arrays)
            refs.insert(at, refs.pop(at + len(outs)))
        forward_kernel(kind, steps, *refs)

    results = list(call(kernel, outs, scratch, scalars, arrays))
    narrow = results.pop(0) if keep else None
    out, *bases = results
    return narrow, out, bases[:3], bases[3:]


def backward(kind, steps, scalars, block, bases, known=None, wanted=()):
    fields = block.shape[0]
    arrays = exchange(block) + [array for base in bases for array in base]
    arrays += [] if known is None else [known]
    shapes = {"narrow": region(4, False), "out": BLOCK_SHAPE, "after": BLOCK_SHAPE, "sums": SUMS_SHAPE, "other": SUMS_SHAPE}
    names = [name for name in shapes if name in ("out", "sums") + tuple(wanted)]
    scratch = [region(fields, True), region(4, False), TOTAL_SHAPE]
    for wide in (True, False):
        scratch += [region(6, wide), region(6, wide, 1), edge_region(wide)]
    if fields == 8:
        scratch += [region(6, True), *base_shapes(True)]
    if "narrow" not in names:
        scratch.append(shapes["narrow"])

    def kernel(*refs):
        refs = list(refs)
        inputs, refs = refs[:2 + len(arrays)], refs[2 + len(arrays):]
        results = dict(zip(names, refs))
        refs = refs[len(names):]
        if "narrow" not in names:
            results["narrow"] = refs.pop()
        backward_kernel(kind, steps, *inputs, *[results.get(name) for name in shapes], *refs)

    return dict(zip(names, call(kernel, [shapes[name] for name in names], scratch, scalars, arrays)))


def last(scalars, block, base, after, sums):
    scratch = [region(4, True), TOTAL_SHAPE, region(6, False), region(6, False, 1), edge_region(False),
               BLOCK_SHAPE, array_of(8 * BLOCK, 2 * HALF), SUMS_SHAPE, array_of(HALF, HALF)]
    outs = [HOME_SHAPE, array_of(256, 1, HALF)]
    return call(last_kernel, outs, scratch, scalars, [*exchange(block), *base, after, *sums])


def on_device(link_angles, cotangent, square_weight, oblong_weight):
    core = lax.axis_index("ta") % 2
    scalars = (core.reshape(1).astype(jnp.int32), jnp.concatenate([square_weight, oblong_weight], 1))
    own, = call(first_kernel, [array_of(8, 2, BLOCK, 2 * HALF)], [array_of(16 * BLOCK, 2 * HALF)], (), (link_angles, cotangent))
    own = permute(own, lambda t, x, c: (t, x, c), home, place)
    other = swap_cores(own)
    chip = jnp.concatenate([jnp.where(core == 0, own, other), jnp.where(core == 0, other, own)], 1)

    w1, b2, base_0, base_1 = forward(0, (0, 0), scalars, chip[:4])
    w3, b4, base_2, base_3 = forward(1, (0, 1), scalars, b2, w1)
    _, b6, base_4, base_5 = forward(2, (1, 1), scalars, b4, w3, False)
    _, b8, base_6, base_7 = forward(0, (2, 2), scalars, b6, None, False)

    two = backward(0, (2, 2), scalars, jnp.concatenate([b8, chip[4:]], 0), (base_7,), None, ("narrow",))
    mix = backward(1, (2, 1), scalars, two["out"], (base_6, base_5), two["narrow"], ("narrow", "other"))
    one = backward(2, (1, 1), scalars, mix["out"], (base_4, base_3), mix["narrow"])
    zero = backward(0, (0, 0), scalars, one["out"], (base_2, base_1), None, ("after",))
    sums = (zero["sums"], one["sums"], mix["other"], mix["sums"], two["sums"])
    result, rows = last(scalars, zero["out"], base_0, zero["after"], sums)

    result = permute(result, lambda t, x, c: (t, x, c), place, home)
    rows = lax.all_to_all(rows, ("ta", "gx"), 0, 0, tiled=True)
    sites = 16 * 8 * BLOCK * BLOCK * 2 * HALF
    totals = (jnp.sum(rows, (0, 1))[:54] * (1.0 / math.sqrt(sites))).reshape(STEPS, 18)
    return result, totals[:, :6], totals[:, 6:]


def solution(mesh):
    in_specs = (P(None, "ta", "gx", None), P(None, "ta", "gx", None), P(), P())
    out_specs = (P(None, "ta", "gx", None), P(), P())
    return jax.shard_map(on_device, mesh=mesh, in_specs=in_specs, out_specs=out_specs, check_vma=False)
```

```python
import functools
import itertools
import math

import jax
import jax.numpy as jnp
from jax import lax
from jax.experimental import pallas as pl
from jax.experimental.pallas import tpu as pltpu
from jax.sharding import PartitionSpec as P


Z = 16
STEPS = 3
STEP = 0.05
TURN = 2.0 * math.pi
PLANES = [(0, 1), (0, 2), (0, 3), (1, 2), (1, 3), (2, 3)]
BLOCK = 4
HALF = 128
F32 = jnp.float32

SIN = [4.442883014678955, -7.308241367340088, 3.6062889099121094, -0.8457635641098022, 0.10920574516057968]
COS = [1.4142135381698608, -6.978850841522217, 5.7394609451293945, -1.8835629224777222, 0.31069815158843994]


def oblong_index(first, second):
    return 6 + first * 3 + second - int(second > first)


def home(tau, xi, core):
    return ((tau % 16) * 2 + core) * 8 + xi % 8


def place(tau, xi, core):
    p = (tau + 12) % 16
    z, y_hi = (p, 0) if p < 8 else (15 - p, 1)
    xi = xi % 8
    x, side = (xi, 0) if xi < 4 else (7 - xi, 1)
    y_lo = side if y_hi == 0 else 1 - side
    return (z * 4 + y_hi * 2 + core) * 8 + y_lo * 4 + x


EVERY = [(t, x, c) for t in range(16) for x in range(8) for c in range(2)]


def permute(array, source, start=place, end=place):
    pairs = [(start(*source(t, x, c)), end(t, x, c)) for t, x, c in EVERY]
    return lax.ppermute(array, ("ta", "gx"), pairs)


def swap_cores(array):
    return permute(array, lambda t, x, c: (t, x, 1 - c))


SOURCES = [((-1, -1), (1, 1)), ((1, -1), (-1, 1)), ((0, -1), (0, 1)), ((-1, 0), (1, 0))]


def exchange(block):
    mine = []
    for choices in SOURCES:
        def source(t, x, c, choices=choices):
            return (t + choices[c][0], x + choices[c][1], 1 - c)
        mine.append(permute(block, source))
    mine = [mine[3], mine[2], jnp.concatenate(mine[:2], 1)]
    return [block, *mine, *[swap_cores(part) for part in mine]]


WIDE = 3


def roll(v, amount, axis):
    axis = axis % v.ndim
    return pltpu.roll(v, amount % v.shape[axis], axis)


def sublane(v):
    return lax.broadcasted_iota(jnp.int32, v.shape, v.ndim - 2)


def step_t(one, two):
    tiles = [one[1:2], two[0:1]]
    if one.shape[0] == WIDE:
        a, b = one[2:], two[2:]
        tiles.append(roll(jnp.where(sublane(a) < 4, b, a), 4, -2))
    return jnp.concatenate(tiles, 0)


def step_x(v, amount):
    if v.shape[0] != WIDE:
        return roll(v, -amount, -2)
    even, odd, rest = v[0:1], v[1:2], v[2:]
    at = sublane(rest)
    if amount > 0:
        moved = roll(rest, -1, -2)
        return jnp.concatenate([
            jnp.where(at == 7, moved, roll(even, -1, -2)),
            jnp.where(at == 7, roll(rest, 3, -2), roll(odd, -1, -2)),
            moved], 0)
    moved = roll(even, 1, -2)
    last = jnp.where(at == 4, roll(odd, -3, -2), roll(rest, 1, -2))
    return jnp.concatenate([moved, roll(odd, 1, -2), jnp.where(at == 0, moved, last)], 0)


def step_y(v, amount):
    yy = lax.broadcasted_iota(jnp.int32, v.shape, v.ndim - 1) % 8
    stays = yy < 7 if amount > 0 else yy > 0
    return jnp.where(stays, roll(v, -amount, -1), roll(v, 7 * amount, -1))


def shift(v, direction, amount):
    if direction == 1:
        return step_x(v, amount)
    if direction == 3:
        return roll(v, -8 * amount, -1)
    even, odd = v[:, 0], v[:, 1]
    if amount > 0:
        return jnp.stack([odd, step_y(even, 1)], 1)
    return jnp.stack([step_y(odd, -1), even], 1)


def narrowed(v):
    even, odd, rest = v[0:1], v[1:2], v[2:]
    inside = sublane(rest) < 6
    return jnp.concatenate([
        jnp.where(inside, roll(even, -2, -2), roll(rest, 6, -2)),
        jnp.where(inside, roll(odd, -2, -2), roll(rest, 2, -2))], 0)


def inner(v):
    return roll(v, -2, -2)[:, :, :BLOCK]


def sin_cos(turns):
    r = turns - jnp.round(turns)
    u = r * r
    s = SIN[-1]
    for a in SIN[-2::-1]:
        s = s * u + a
    c = COS[-1]
    for a in COS[-2::-1]:
        c = c * u + a
    s = s * r
    return s * c, 1.0 - s * s


def curls(here, ahead):
    for m, k in PLANES:
        moved = step_t(here[k], ahead[k]) if m == 0 else shift(here[k], m, 1)
        yield (here[m] - shift(here[m], k, 1)) + (moved - here[k])


def directions(j):
    m, k = PLANES[j]
    return [(m, oblong_index(m, k)), (k, oblong_index(k, m))]


def loop(first, last, body):
    def turn(p, carry):
        body(p)
        return carry

    if last > first:
        lax.fori_loop(first, last, turn, 0)


def run(*passes, together=True):
    for _ in itertools.zip_longest(*passes) if together else itertools.chain(*passes):
        pass


def schedule(pairs, own, first, second, third):
    def step(is_own, p, has_first, has_third):
        passes = [third(p - 1)] if has_third else []
        passes.append(second(is_own, p))
        if has_first:
            passes.append(first(p + 2))
        run(*passes, together=has_first and pairs == WIDE_PAIRS)

    loop(0, 2, lambda p: run(first(p)))
    ranges = {}
    for p in range(pairs - 1):
        key = (own <= p < own + 2, p + 2 < pairs, third is not None and p >= 2)
        ranges.setdefault(key, []).append(p)
    for (is_own, has_first, has_third), at in ranges.items():
        loop(at[0], at[-1] + 1, lambda p, k=(is_own, has_first, has_third): step(k[0], p, k[1], k[2]))
    if third is not None:
        run(third(pairs - 2))


def add_back(total, value, j, direction, edge, weight):
    if direction == 0:
        back = step_t(edge[j], value)
        edge[j] = value
    else:
        back = shift(value, direction, -1)
    return total + weight * (value + back)


def base_pass(pairs, own, read, weights, sin, cos, cosines, sines, force=None, edge=None, write=None):
    def plaquettes(p):
        here = [read(d, p) for d in range(4)]
        ahead = [read(d, jnp.minimum(p + 1, pairs - 1)) for d in range(4)]
        for j, angle in enumerate(curls(here, ahead)):
            sin[j, p], cos[j, p] = sin_cos(angle)
            yield

    def forces(is_own, p):
        for j in range(6):
            s, c = sin[j, p], cos[j, p]
            if force is not None:
                total = weights[j] * s
            if is_own:
                sines[j, p - own] = s[:2]
            for direction, index in directions(j):
                if direction == 0:
                    s2, c2 = step_t(s, sin[j, p + 1]), step_t(c, cos[j, p + 1])
                else:
                    s2, c2 = shift(s, direction, 1), shift(c, direction, 1)
                cosines[index - 6, p] = c * c2 - s * s2
                if is_own or force is not None:
                    value = s * c2 + c * s2
                if is_own:
                    sines[index, p - own] = value[:2]
                if force is not None:
                    total = add_back(total, value, j, direction, edge, weights[index])
            if force is not None:
                force[j, p] = total
            yield

    schedule(pairs, own, plaquettes, forces, None if force is None else link_pass(force, write))


def vector_pass(pairs, own, read, weights, cos_at, cosines_at, sines_at, vec, force, edge, total, write):
    def plaquettes(p):
        here = [read(d, p) for d in range(4)]
        ahead = [read(d, jnp.minimum(p + 1, pairs - 1)) for d in range(4)]
        for j, value in enumerate(curls(here, ahead)):
            vec[j, p] = value
            yield

    total[...] = jnp.zeros(total.shape, F32)

    def forces(is_own, p):
        for j in range(6):
            q = vec[j, p]
            result = weights[j] * (cos_at(j, p) * q)
            if is_own:
                total[j] += jnp.sum(sines_at(j, p - own) * q[:2], 0)
            for direction, index in directions(j):
                both = q + (step_t(q, vec[j, p + 1]) if direction == 0 else shift(q, direction, 1))
                if is_own:
                    total[index] += jnp.sum(sines_at(index, p - own) * both[:2], 0)
                value = cosines_at(index - 6, p) * both
                result = add_back(result, value, j, direction, edge, weights[index])
            force[j, p] = result
            yield

    schedule(pairs, own, plaquettes, forces, link_pass(force, write))


def link_pass(force, write):
    def links(p):
        parts = [None] * 4
        for j, (m, k) in enumerate(PLANES):
            h = force[j, p]
            back_m = step_t(force[j, p - 1], h) if m == 0 else shift(h, m, -1)
            first, second = shift(h, k, -1) - h, h - back_m
            parts[m] = first if parts[m] is None else parts[m] + first
            parts[k] = second if parts[k] is None else parts[k] + second
            yield
        write(p, parts)

    return links


WIDE_PAIRS = 6
NARROW_PAIRS = 4


def region(fields, wide, cut=0):
    pairs, tiles = (WIDE_PAIRS, WIDE) if wide else (NARROW_PAIRS, 2)
    return jax.ShapeDtypeStruct((fields, pairs - cut, tiles, 2, 8, HALF), F32)


def edge_region(wide):
    return jax.ShapeDtypeStruct((3, WIDE if wide else 2, 2, 8, HALF), F32)


def array_of(*shape):
    return jax.ShapeDtypeStruct(shape, F32)


HOME_SHAPE = array_of(4, 2, BLOCK, 2 * HALF)
BLOCK_SHAPE = array_of(4, BLOCK, BLOCK, 2 * HALF)
OWN_SHAPE = array_of(18, 2, 2, 2, 8, HALF)
SUMS_SHAPE = array_of(18, 8, HALF)
TOTAL_SHAPE = array_of(18, 2, 8, HALF)


def relabelled(rows, back):
    old = lax.broadcasted_iota(jnp.int32, (2 * HALF, 2 * HALF), 1 if back else 0)
    new = lax.broadcasted_iota(jnp.int32, (2 * HALF, 2 * HALF), 0 if back else 1)
    y, z = 2 * (new % 8) + new // HALF, (new % HALF) // 8
    matrix = jnp.where(old == y * Z + z, 1.0, 0.0).astype(F32)
    return lax.dot(rows, matrix, precision=lax.Precision.HIGHEST, preferred_element_type=F32)


def first_kernel(links, cotangent, out, rows):
    for f in range(8):
        for t in range(2):
            value = links[f, t] * (1.0 / TURN) if f < 4 else cotangent[f - 4, t]
            rows[(2 * f + t) * BLOCK:(2 * f + t + 1) * BLOCK] = value
    rows[...] = relabelled(rows[...], False)
    for f in range(8):
        for t in range(2):
            out[f, t] = rows[(2 * f + t) * BLOCK:(2 * f + t + 1) * BLOCK]


def assemble(core, blocks, wide):
    def put(row, column, block, first=0):
        for i in range(BLOCK):
            odd = i % 2
            tile = odd if column < 2 else 2
            x = BLOCK * (column if column < 2 else odd)
            for h in range(2):
                part = block[:, first + i, :, h * HALF:(h + 1) * HALF]
                wide[:, 2 * row + i // 2, tile, h, x:x + BLOCK, :] = part

    def fill(left, right):
        where = ((2, 0), (2, BLOCK), (1, 0), (0, 0))
        for (i, first), row, column in zip(where, (0, 2, 1, 0), (0, 0, 0, 1)):
            put(row, column, left[i], first)
        for (i, first), row, column in zip(where, (2, 0, 1, 2), (2, 2, 2, 1)):
            put(row, column, right[i], first)

    put(1, 1, blocks[0])

    @pl.when(core == 0)
    def _():
        fill(blocks[1:4], blocks[4:])

    @pl.when(core != 0)
    def _():
        fill(blocks[4:], blocks[1:4])


def rows_of(ref, first=0):
    return lambda d, p: ref[first + d, p]


def crop_of(ref, first=0):
    return lambda d, p: narrowed(ref[first + d, p + 1])


def put_block(out, d, p, v):
    at = pl.ds(2 * p - 2, 2)
    v = inner(v)
    out[d, at, :, :HALF] = v[:, 0]
    out[d, at, :, HALF:] = v[:, 1]


def row_weights(weights, step):
    return [weights[step, j] for j in range(18)]


def forward_kernel(kind, steps, core, weights, *rest):
    blocks, rest = rest[:7], list(rest[7:])
    previous = rest.pop(0) if kind else None
    narrow, out, cos_w, cosines_w, sines_w, cos_n, cosines_n, sines_n = rest[:8]
    wide, drift, sin_w, force_w, edge_w, sin_n, force_n, edge_n = rest[8:]
    assemble(core[0], blocks, wide)
    crop = crop_of(wide)
    unit = STEP / TURN

    def write_wide(p, parts):
        q = p - 1
        for d in range(4):
            z = narrowed(parts[d]) * unit
            if kind == 0:
                drift[d, q] = z
                narrow[d, q] = crop(d, q) + 0.25 * z
            elif kind == 1:
                narrow[d, q] = previous[d, q] + 0.75 * z
            else:
                second = crop(d, q)
                narrow[d, q] = second + 8.0 / 9.0 * z - 17.0 / 9.0 * (second - previous[d, q])

    base_pass(WIDE_PAIRS, 2, rows_of(wide), row_weights(weights, steps[0]),
              sin_w, cos_w, cosines_w, sines_w, force_w, edge_w, write_wide)

    def write_narrow(p, parts):
        for d in range(4):
            z = parts[d] * unit
            if kind == 0:
                value = narrow[d, p] + 8.0 / 9.0 * z - 17.0 / 36.0 * drift[d, p]
            elif kind == 1:
                value = narrow[d, p] + 0.25 * z
            else:
                value = crop(d, p) + 0.75 * z
            put_block(out, d, p, value)

    base_pass(NARROW_PAIRS, 1, rows_of(narrow), row_weights(weights, steps[1]),
              sin_n, cos_n, cosines_n, sines_n, force_n, edge_n, write_narrow)


def put_sums(out, total, first, factor, add=False):
    x = lax.broadcasted_iota(jnp.int32, (8, HALF), 0)
    kept = (x >= first) & (x < first + BLOCK)
    for index in range(18):
        value = jnp.where(kept, (total[index, 0] + total[index, 1]) * factor, 0.0)
        out[index] = out[index] + value if add else value


def readers(base):
    return [rows_of(ref) for ref in base]


def backward_kernel(kind, steps, core, weights, *rest):
    blocks, rest = rest[:7], list(rest[7:])
    first = blocks[0].shape[0] - 4
    base_w = None if first else [rest.pop(0) for _ in range(3)]
    base_n = [rest.pop(0) for _ in range(3)]
    known = rest.pop(0) if kind else None
    narrow, out, after_out, sums, other_sums = [rest.pop(0) for _ in range(5)]
    wide, keep, total, vec_w, force_w, edge_w, vec_n, force_n, edge_n, *base_scratch = rest
    assemble(core[0], blocks, wide)
    row = row_weights(weights, steps[0])
    if first:
        sin_w, *base_w = base_scratch
        base_pass(WIDE_PAIRS, 2, rows_of(wide), row, sin_w, *base_w)
    crop = crop_of(wide, first)
    factor = (0.75, 1.0, 8.0 / 9.0)[kind]

    def write_wide(p, parts):
        q = p - 1
        for d in range(4):
            image = narrowed(parts[d]) * (STEP * factor)
            source = crop(d, q)
            if kind == 0:
                narrow[d, q] = image
                keep[d, q] = source + image
            elif kind == 1:
                narrow[d, q] = 4.0 * source + 17.0 / 9.0 * known[d, q] + image
            else:
                after = known[d, q] + source + image
                keep[d, q] = after
                narrow[d, q] = 0.25 * after - 17.0 / 36.0 * source

    vector_pass(WIDE_PAIRS, 2, rows_of(wide, first), row, *readers(base_w),
                vec_w, force_w, edge_w, total, write_wide)
    put_sums(sums, total, BLOCK, factor)
    factor_two = (8.0 / 9.0, 0.75, 1.0)[kind]

    def write_narrow(p, parts):
        for d in range(4):
            image = parts[d] * (STEP * factor_two)
            if kind == 0:
                after = keep[d, p] + image
                value = 0.25 * after - 17.0 / 36.0 * narrow[d, p]
                if after_out is not None:
                    put_block(after_out, d, p, after)
            elif kind == 1:
                value = image
            else:
                value = keep[d, p] + image
            put_block(out, d, p, value)

    vector_pass(NARROW_PAIRS, 1, rows_of(narrow), row_weights(weights, steps[1]), *readers(base_n),
                vec_n, force_n, edge_n, total, write_narrow)
    if other_sums is None:
        put_sums(sums, total, 2, factor_two, True)
    else:
        put_sums(other_sums, total, 2, factor_two)


def last_kernel(core, weights, *rest):
    blocks, rest = rest[:7], rest[7:]
    cos, cosines, sines, after, zero, one, mix_one, mix_two, two = rest[:9]
    out, sent, wide, total, vec, force, edge, block, rows, sums, terms = rest[9:]
    assemble(core[0], blocks, wide)

    def sines_at(index, i):
        return roll(sines[index, i], -2, -2)

    def write(p, parts):
        for d in range(4):
            put_block(block, d, p, parts[d] * STEP)

    vector_pass(NARROW_PAIRS, 1, crop_of(wide), row_weights(weights, 0), crop_of(cos), crop_of(cosines), sines_at,
                vec, force, edge, total, write)
    put_sums(sums, total, 2, 1.0)
    terms[...] = jnp.zeros(terms.shape, F32)
    for step, parts in enumerate(((sums, zero), (one, mix_one), (two, mix_two))):
        both = parts[0][...] + parts[1][...]
        terms[18 * step:18 * step + 18, :] = jnp.sum(both, 1) * (-0.5 * STEP)
    row = lax.dot_general(jnp.ones((8, HALF), F32), terms[...], (((1,), (1,)), ((), ())),
                          precision=lax.Precision.HIGHEST, preferred_element_type=F32)
    sent[...] = jnp.broadcast_to(row[None, :1], sent.shape)

    def finish(first):
        for d in range(4):
            for t in range(2):
                at = (2 * d + t) * BLOCK
                rows[at:at + BLOCK] = block[d, first + t] + after[d, first + t]
        rows[...] = relabelled(rows[...], True)
        for d in range(4):
            for t in range(2):
                at = (2 * d + t) * BLOCK
                out[d, t] = rows[at:at + BLOCK]

    @pl.when(core[0] == 0)
    def _():
        finish(0)

    @pl.when(core[0] != 0)
    def _():
        finish(2)


VMEM = pl.BlockSpec(memory_space=pltpu.VMEM)
SMEM = pl.BlockSpec(memory_space=pltpu.SMEM)


def call(kernel, outs, scratch, scalars, arrays):
    return pl.pallas_call(
        kernel,
        out_shape=outs,
        in_specs=[SMEM] * len(scalars) + [VMEM] * len(arrays),
        out_specs=[VMEM] * len(outs),
        scratch_shapes=[pltpu.VMEM(shape.shape, F32) for shape in scratch],
        compiler_params=pltpu.CompilerParams(vmem_limit_bytes=18 * 2**20),
    )(*scalars, *arrays)


def base_shapes(wide):
    return [region(6, wide), region(12, wide, 1), OWN_SHAPE]


def forward(kind, steps, scalars, block, previous=None, keep=True):
    arrays = exchange(block) + ([] if previous is None else [previous])
    outs = [BLOCK_SHAPE, *base_shapes(True), *base_shapes(False)]
    scratch = [region(4, True), region(4, False)]
    for wide in (True, False):
        scratch += [region(6, wide), region(6, wide, 1), edge_region(wide)]
    if keep:
        outs = [region(4, False)] + outs
    else:
        scratch = [region(4, False)] + scratch

    def kernel(*refs):
        refs = list(refs)
        if not keep:
            at = 2 + len(arrays)
            refs.insert(at, refs.pop(at + len(outs)))
        forward_kernel(kind, steps, *refs)

    results = list(call(kernel, outs, scratch, scalars, arrays))
    narrow = results.pop(0) if keep else None
    out, *bases = results
    return narrow, out, bases[:3], bases[3:]


def backward(kind, steps, scalars, block, bases, known=None, wanted=()):
    fields = block.shape[0]
    arrays = exchange(block) + [array for base in bases for array in base]
    arrays += [] if known is None else [known]
    shapes = {"narrow": region(4, False), "out": BLOCK_SHAPE, "after": BLOCK_SHAPE, "sums": SUMS_SHAPE, "other": SUMS_SHAPE}
    names = [name for name in shapes if name in ("out", "sums") + tuple(wanted)]
    scratch = [region(fields, True), region(4, False), TOTAL_SHAPE]
    for wide in (True, False):
        scratch += [region(6, wide), region(6, wide, 1), edge_region(wide)]
    if fields == 8:
        scratch += [region(6, True), *base_shapes(True)]
    if "narrow" not in names:
        scratch.append(shapes["narrow"])

    def kernel(*refs):
        refs = list(refs)
        inputs, refs = refs[:2 + len(arrays)], refs[2 + len(arrays):]
        results = dict(zip(names, refs))
        refs = refs[len(names):]
        if "narrow" not in names:
            results["narrow"] = refs.pop()
        backward_kernel(kind, steps, *inputs, *[results.get(name) for name in shapes], *refs)

    return dict(zip(names, call(kernel, [shapes[name] for name in names], scratch, scalars, arrays)))


def last(scalars, block, base, after, sums):
    scratch = [region(4, True), TOTAL_SHAPE, region(6, False), region(6, False, 1), edge_region(False),
               BLOCK_SHAPE, array_of(8 * BLOCK, 2 * HALF), SUMS_SHAPE, array_of(HALF, HALF)]
    outs = [HOME_SHAPE, array_of(256, 1, HALF)]
    return call(last_kernel, outs, scratch, scalars, [*exchange(block), *base, after, *sums])


def on_device(link_angles, cotangent, square_weight, oblong_weight):
    core = lax.axis_index("ta") % 2
    scalars = (core.reshape(1).astype(jnp.int32), jnp.concatenate([square_weight, oblong_weight], 1))
    own, = call(first_kernel, [array_of(8, 2, BLOCK, 2 * HALF)], [array_of(16 * BLOCK, 2 * HALF)], (), (link_angles, cotangent))
    own = permute(own, lambda t, x, c: (t, x, c), home, place)
    other = swap_cores(own)
    chip = jnp.concatenate([jnp.where(core == 0, own, other), jnp.where(core == 0, other, own)], 1)

    w1, b2, base_0, base_1 = forward(0, (0, 0), scalars, chip[:4])
    w3, b4, base_2, base_3 = forward(1, (0, 1), scalars, b2, w1)
    _, b6, base_4, base_5 = forward(2, (1, 1), scalars, b4, w3, False)
    _, b8, base_6, base_7 = forward(0, (2, 2), scalars, b6, None, False)

    two = backward(0, (2, 2), scalars, jnp.concatenate([b8, chip[4:]], 0), (base_7,), None, ("narrow",))
    mix = backward(1, (2, 1), scalars, two["out"], (base_6, base_5), two["narrow"], ("narrow", "other"))
    one = backward(2, (1, 1), scalars, mix["out"], (base_4, base_3), mix["narrow"])
    zero = backward(0, (0, 0), scalars, one["out"], (base_2, base_1), None, ("after",))
    sums = (zero["sums"], one["sums"], mix["other"], mix["sums"], two["sums"])
    result, rows = last(scalars, zero["out"], base_0, zero["after"], sums)

    result = permute(result, lambda t, x, c: (t, x, c), place, home)
    rows = lax.all_to_all(rows, ("ta", "gx"), 0, 0, tiled=True)
    sites = 16 * 8 * BLOCK * BLOCK * 2 * HALF
    totals = (jnp.sum(rows, (0, 1))[:54] * (1.0 / math.sqrt(sites))).reshape(STEPS, 18)
    return result, totals[:, :6], totals[:, 6:]


def solution(mesh):
    in_specs = (P(None, "ta", "gx", None), P(None, "ta", "gx", None), P(), P())
    out_specs = (P(None, "ta", "gx", None), P(), P())
    return jax.shard_map(on_device, mesh=mesh, in_specs=in_specs, out_specs=out_specs, check_vma=False)
```
